256 devices in a mesh: dp: 64 (over z_lo, y, x), mp: 4 (over z_hi, core).
Axes of the slice: x: 4, y: 4, z: 8 (z_hi: 2, z_lo: 4; z = z_hi * 4 + z_lo), core: 2. Of those that a mesh axis runs over, the one named last changes fastest.
Arguments:
- view_one: bfloat16 [8192, 4096], P('dp', 'mp'), may hold values from -400 to 400
- view_two: bfloat16 [8192, 4096], P('dp', 'mp'), may hold values from -400 to 400
- proj_weight: bfloat16 [4096, 4096], P(None, 'mp'), may hold values from -0.09375 to 0.09375
Outputs:
- grad_one: bfloat16 [8192, 4096], P('dp', 'mp')
- grad_two: bfloat16 [8192, 4096], P('dp', 'mp')
The draws below stay inside these ranges and needn't reach their ends.
All inputs are finite; a program needn't handle non-finite values.
Results may differ from the reference program's by a relative error of at most 0.025.
Values may be sent and summed in bfloat16 or wider, within the bound.
No kernel may reach another device: no remote copies, remote signals or barrier semaphores. Data moves between devices by JAX's collectives and lax.ppermute only.
A program may use at most 128 MiB of HBM per device.

```python
import math
import jax
import jax.numpy as jnp
from jax import lax

E = 4096
K = 4096
B = 8192
N_MP = 4


def shared_parts(key):
    rows_key, cols_key, base_key = jax.random.split(key, 3)
    position = jnp.arange(B, dtype=jnp.float32)[:, None]
    rise = 1.0 + 2.0 * position / (B - 1)
    spread = jnp.exp(jax.random.uniform(rows_key, (B, 1), jnp.float32, 0.0, math.log(10.0)))
    column_scale = jnp.exp(jax.random.uniform(cols_key, (1, E), jnp.float32, math.log(0.3), math.log(3.0)))
    normal_base = jnp.clip(jax.random.normal(base_key, (B, E), jnp.float32), -4.0, 4.0)
    return (rise * spread, column_scale, normal_base)


def compose(key, row_scale, column_scale, base):
    return jnp.clip(row_scale * column_scale * base, -400.0, 400.0)


def draw_view_one(key, part):
    row_scale, column_scale, normal_base = shared_parts(key)
    key = jax.random.fold_in(key, 11)
    value = compose(key, row_scale, column_scale, normal_base)
    return value.astype(jnp.bfloat16)


def draw_view_two(key, part):
    row_scale, column_scale, normal_base = shared_parts(key)
    key = jax.random.fold_in(key, 12)
    own_key, col_key, off_key = jax.random.split(key, 3)
    second_scale = jnp.exp(jax.random.uniform(col_key, (1, E), jnp.float32, math.log(0.3), math.log(3.0)))
    noise = jnp.clip(jax.random.normal(own_key, (B, E), jnp.float32), -4.0, 4.0)
    value = compose(off_key, row_scale, second_scale, 0.8 * normal_base + 0.6 * noise)
    return value.astype(jnp.bfloat16)


def levels(key, shape, cuts, smallest, top_value):
    level = 1.0
    for axis_at, shards_of in cuts:
        heights = jax.random.uniform(jax.random.fold_in(jax.random.fold_in(key, 6), axis_at), (shards_of,), jnp.float32, smallest / len(cuts), top_value / len(cuts))
        level = level * jnp.repeat(jnp.exp(heights), shape[axis_at] // shards_of).reshape((-1,) + (1,) * (len(shape) - 1 - axis_at))
    return level


def gaussian(rng, shape, width, most, shards=(), kind=jnp.bfloat16):
    values = jax.random.normal(rng, shape, jnp.float32) * width
    if len(shards) > 0:
        values = levels(rng, shape, shards, -0.22, 0.18) * values
    return jnp.clip(values, min=-most, max=most).astype(kind)


def setup_inputs(seed: int = 0) -> dict:
    key_list = jax.random.split(jax.random.key(seed), 4)
    view_one = draw_view_one(jax.random.fold_in(key_list[3], 71), 0)
    view_two = draw_view_two(jax.random.fold_in(key_list[3], 71), 0)
    proj_weight = gaussian(key_list[2], (K, E), E ** -0.5, 0.09375, ((1, 4),))
    return {"view_one": view_one, "view_two": view_two, "proj_weight": proj_weight}


OFF_WEIGHT = 0.0125
EPSILON = 1e-05

def normalize(view):
    values = view.astype(jnp.float32)
    center = lax.optimization_barrier(jnp.mean(values, axis=0))
    centered = values - center
    variance = lax.optimization_barrier(jnp.mean(centered * centered, axis=0))
    inverse = lax.rsqrt(variance + EPSILON)
    return ((centered * inverse).astype(jnp.bfloat16), inverse)

def norm_backward(upstream, normed, inverse):
    normal_values = normed.astype(jnp.float32)
    mean_up = lax.optimization_barrier(jnp.mean(upstream, axis=0))
    mean_cross = lax.optimization_barrier(jnp.mean(upstream * normal_values, axis=0))
    return (inverse * (upstream - mean_up - normal_values * mean_cross)).astype(jnp.bfloat16)

def input_grad(delta, proj_weight):
    block = E // N_MP
    total = jnp.zeros((delta.shape[0], proj_weight.shape[0]), jnp.float32)
    for member in range(N_MP):
        piece = jnp.dot(delta[:, member * block:(member + 1) * block], proj_weight[:, member * block:(member + 1) * block].T, preferred_element_type=jnp.float32).astype(jnp.bfloat16)
        piece = lax.optimization_barrier(piece)
        total = total + piece.astype(jnp.float32)
    return total.astype(jnp.bfloat16)

def reference(view_one, view_two, proj_weight):
    row_count = view_one.shape[0]
    norm_one, inverse_one = normalize(view_one)
    norm_two, inverse_two = normalize(view_two)
    corr = jnp.dot(norm_one.T, norm_two, preferred_element_type=jnp.float32) / row_count
    row_ids = lax.broadcasted_iota(jnp.int32, (E, E), 0)
    col_ids = lax.broadcasted_iota(jnp.int32, (E, E), 1)
    grad_corr = jnp.where(row_ids == col_ids, -2.0 * (1.0 - corr), 2.0 * OFF_WEIGHT * corr).astype(jnp.bfloat16)
    up_one = jnp.dot(norm_two, grad_corr.T, preferred_element_type=jnp.float32)
    up_two = jnp.dot(norm_one, grad_corr, preferred_element_type=jnp.float32)
    delta_one = norm_backward(up_one, norm_one, inverse_one)
    delta_two = norm_backward(up_two, norm_two, inverse_two)
    return (input_grad(delta_one, proj_weight), input_grad(delta_two, proj_weight))
```

```python
import jax
import jax.numpy as jnp
from jax import lax
from jax.sharding import Mesh, PartitionSpec as P

OFF_WEIGHT = 0.0125
EPSILON = 1e-05
F32 = jnp.float32
BF16 = jnp.bfloat16
PLANE = ("y", "x")
SWAP = [(0, 1), (1, 0)]
EXTRA = 16


def dot(left, right, left_dim, right_dim):
    return lax.dot_general(
        left, right, (((left_dim,), (right_dim,)), ((), ())), preferred_element_type=F32
    )


def swap(value, axis):
    return lax.ppermute(value, axis, SWAP)


def gather_zl(value):
    count = lax.axis_size("zl")
    return lax.all_to_all(
        jnp.broadcast_to(value[None], (count,) + value.shape), "zl", 0, 0, tiled=True
    )


def small_gather_zl(value):
    count = lax.axis_size("zl")
    parts = [value]
    for shift in range(1, count):
        parts.append(lax.ppermute(value, "zl", [(i, (i + shift) % count) for i in range(count)]))
    return parts


def moments(values, total_rows):
    rows = values.shape[0]
    wide = values.astype(F32)
    mean = jnp.sum(wide, axis=0) / rows
    square = jnp.sum((wide - mean) ** 2, axis=0)
    parts = small_gather_zl(jnp.stack([mean, square]))
    center = sum(p[0] for p in parts) * (rows / total_rows)
    total = sum(p[1] + rows * (p[0] - center) ** 2 for p in parts)
    return center, lax.rsqrt(total / total_rows + EPSILON)


def split(vector):
    high = vector.astype(BF16)
    return high, (vector - high.astype(F32)).astype(BF16)


def extra_rows(vectors, width):
    rows = []
    for vector in vectors:
        rows.extend(split(vector))
    stacked = jnp.stack(rows)
    return jnp.pad(stacked, ((0, EXTRA - stacked.shape[0]), (0, 0)))


def local(view_one, view_two, proj_weight):
    rows, width = view_one.shape
    n_zl, n_y, n_x = lax.axis_size("zl"), lax.axis_size("y"), lax.axis_size("x")
    n_plane = n_y * n_x
    total_rows = rows * n_zl * n_plane
    blk_i, blk_j = width // n_x, width // n_y
    core = lax.axis_index("c")
    zh = lax.axis_index("zh")

    crossed = swap(view_two, "zh")
    send_one = view_one.reshape(rows, n_x, blk_i).transpose(1, 0, 2)
    send_one = jnp.broadcast_to(send_one[None], (n_y, n_x, rows, blk_i)).reshape(n_plane, rows, blk_i)
    own_one = lax.all_to_all(send_one, PLANE, 0, 0, tiled=True).reshape(n_plane * rows, blk_i)
    both = jnp.concatenate(
        [view_two.reshape(rows, n_y, blk_j), crossed.reshape(rows, n_y, blk_j)], axis=2
    ).transpose(1, 0, 2)
    both = jnp.broadcast_to(both[:, None], (n_y, n_x, rows, 2 * blk_j)).reshape(n_plane, rows, 2 * blk_j)
    plane_two = lax.all_to_all(both, PLANE, 0, 0, tiled=True).reshape(n_plane * rows, 2 * blk_j)
    plane_one = jnp.concatenate([own_one, swap(own_one, "c")], axis=1)

    mean_one, rstd_one = moments(plane_one, total_rows)
    mean_two, rstd_two = moments(plane_two, total_rows)
    norm_one = ((plane_one.astype(F32) - mean_one) * rstd_one).astype(BF16)
    norm_two = ((plane_two.astype(F32) - mean_two) * rstd_two).astype(BF16)

    tile_i, tile_j = norm_one.shape[1], norm_two.shape[1]
    part = dot(norm_one, norm_two, 0, 0).astype(BF16).reshape(n_zl, tile_i // n_zl, tile_j)
    sums = extra_rows(
        [jnp.sum(norm_one.astype(F32), axis=0), jnp.sum(norm_two.astype(F32), axis=0)], tile_j
    )
    part = jnp.concatenate([part, jnp.broadcast_to(sums[None], (n_zl,) + sums.shape)], axis=1)
    part = jnp.sum(lax.all_to_all(part, "zl", 0, 0, tiled=True).astype(F32), axis=0)
    slice_i = tile_i // n_zl
    mu_one = (part[slice_i] + part[slice_i + 1]) / total_rows
    mu_two = (part[slice_i + 2] + part[slice_i + 3]) / total_rows
    corr = part[:slice_i] / total_rows
    on_diag = lax.axis_index("x") == lax.axis_index("y")

    def diagonal(height, first):
        row_ids = first + lax.broadcasted_iota(jnp.int32, (height, tile_j), 0)
        col_ids = lax.broadcasted_iota(jnp.int32, (height, tile_j), 1)
        return (row_ids == col_ids) & (row_ids < blk_i) & on_diag

    grad = jnp.where(
        diagonal(slice_i, lax.axis_index("zl") * slice_i),
        -2.0 * (1.0 - corr),
        2.0 * OFF_WEIGHT * corr,
    ).astype(BF16)
    grad = gather_zl(grad).reshape(tile_i, tile_j)

    wide = grad.astype(F32)
    product = wide * jnp.where(diagonal(tile_i, 0), 1.0 + 0.5 * wide, wide / (2.0 * OFF_WEIGHT))
    cross_one, mean_up_one = jnp.sum(product, axis=1), jnp.sum(wide * mu_two[None, :], axis=1)
    cross_two, mean_up_two = jnp.sum(product, axis=0), jnp.sum(wide * mu_one[:, None], axis=0)

    def to_rows(upstream, vectors):
        columns = upstream.shape[1]
        extra = extra_rows(vectors, columns)
        slots = upstream.astype(BF16).reshape(n_plane, rows, columns)
        slots = jnp.concatenate([slots, jnp.broadcast_to(extra[None], (n_plane,) + extra.shape)], axis=1)
        return lax.all_to_all(slots, PLANE, 0, 0, tiled=True).reshape(n_y, n_x, rows + EXTRA, columns)

    up_two = dot(norm_one, grad, 1, 0)
    got_two = jnp.sum(to_rows(up_two, [cross_two, mean_up_two]).astype(F32), axis=1)
    cross_two = got_two[:, rows] + got_two[:, rows + 1]
    mean_up_two = got_two[:, rows + 2] + got_two[:, rows + 3]
    cross_sent = jnp.stack(
        split(cross_two[:, blk_j:]) + split(mean_up_two[:, blk_j:])
    ).reshape(4, width)
    up_two = got_two[:, :rows].transpose(1, 0, 2)
    sent = jnp.concatenate(
        [
            up_two[:, :, blk_j:].astype(BF16).reshape(rows, width),
            jnp.pad(cross_sent, ((0, EXTRA - 4), (0, 0))),
        ],
        axis=0,
    )
    sent = swap(sent, "zh").astype(F32)
    up_two = up_two[:, :, :blk_j].reshape(rows, width) + sent[:rows]
    cross_two = cross_two[:, :blk_j].reshape(width) + sent[rows] + sent[rows + 1]
    mean_up_two = mean_up_two[:, :blk_j].reshape(width) + sent[rows + 2] + sent[rows + 3]

    up_one = dot(norm_two, grad, 1, 1)
    other = jnp.concatenate(
        [
            up_one[:, blk_i:].astype(BF16),
            extra_rows([cross_one[blk_i:], mean_up_one[blk_i:]], blk_i),
        ],
        axis=0,
    )
    other = swap(other, "c").astype(F32)
    plane_rows = n_plane * rows
    up_one = up_one[:, :blk_i] + other[:plane_rows]
    tail = other[plane_rows:]
    cross_one = cross_one[:blk_i] + tail[0] + tail[1]
    mean_up_one = mean_up_one[:blk_i] + tail[2] + tail[3]
    got_one = jnp.sum(to_rows(up_one, [cross_one, mean_up_one]).astype(F32), axis=0)
    up_one = got_one[:, :rows].transpose(1, 0, 2).reshape(rows, width)
    cross_one = (got_one[:, rows] + got_one[:, rows + 1]).reshape(width)
    mean_up_one = (got_one[:, rows + 2] + got_one[:, rows + 3]).reshape(width)

    def own_stats(mean, rstd, axis):
        count = lax.axis_size(axis)
        return lax.all_to_all(
            jnp.broadcast_to(jnp.stack([mean, rstd])[None], (count, 2, mean.shape[0])), axis, 0, 0, tiled=True
        )

    stats_one = own_stats(mean_one[:blk_i], rstd_one[:blk_i], "x")
    stats_two = own_stats(mean_two[:blk_j], rstd_two[:blk_j], "y")

    def delta(view, stats, upstream, mean_up, cross):
        mean, rstd = stats[:, 0].reshape(width), stats[:, 1].reshape(width)
        normal = ((view.astype(F32) - mean) * rstd).astype(BF16).astype(F32)
        return (rstd * (upstream - mean_up - normal * cross)).astype(BF16)

    delta_one = delta(view_one, stats_one, up_one, mean_up_one, cross_one)
    delta_two = delta(view_two, stats_two, up_two, mean_up_two, cross_two)

    def input_grad(value):
        part = dot(value, proj_weight, 1, 1).reshape(rows, 2, 2, width)
        keep = lax.dynamic_index_in_dim(part, core, 2, keepdims=False)
        give = lax.dynamic_index_in_dim(part, 1 - core, 2, keepdims=False)
        part = keep + swap(give.astype(BF16), "c").astype(F32)
        keep = lax.dynamic_index_in_dim(part, zh, 1, keepdims=False)
        give = lax.dynamic_index_in_dim(part, 1 - zh, 1, keepdims=False)
        return (keep + swap(give.astype(BF16), "zh").astype(F32)).astype(BF16)

    return input_grad(delta_one), input_grad(delta_two)


def solution(mesh):
    fine = Mesh(mesh.devices.reshape(4, 4, 4, 2, 2), ("zl", "y", "x", "zh", "c"))
    spec = P(("zl", "y", "x"), ("zh", "c"))
    return jax.shard_map(
        local,
        mesh=fine,
        in_specs=(spec, spec, P(None, ("zh", "c"))),
        out_specs=(spec, spec),
        check_vma=False,
    )
```

```python
import jax
import jax.numpy as jnp
from jax import lax
from jax.sharding import Mesh, PartitionSpec as P

OFF_WEIGHT = 0.0125
EPSILON = 1e-05
F32 = jnp.float32
BF16 = jnp.bfloat16
PLANE = ("y", "x")
SWAP = [(0, 1), (1, 0)]
EXTRA = 16


def dot(left, right, left_dim, right_dim):
    return lax.dot_general(
        left, right, (((left_dim,), (right_dim,)), ((), ())), preferred_element_type=F32
    )


def swap(value, axis):
    return lax.ppermute(value, axis, SWAP)


def gather_zl(value):
    count = lax.axis_size("zl")
    return lax.all_to_all(
        jnp.broadcast_to(value[None], (count,) + value.shape), "zl", 0, 0, tiled=True
    )


def small_gather_zl(value):
    count = lax.axis_size("zl")
    parts = [value]
    for shift in range(1, count):
        parts.append(lax.ppermute(value, "zl", [(i, (i + shift) % count) for i in range(count)]))
    return parts


def combine(means, squares, rows):
    mean = sum(means) / len(means)
    return mean, sum(squares) + rows * sum((m - mean) ** 2 for m in means)


def moments(values):
    rows = values.shape[0]
    wide = values.astype(F32)
    mean = jnp.sum(wide, axis=0) / rows
    square = jnp.sum((wide - mean) ** 2, axis=0)
    parts = small_gather_zl(jnp.stack([mean, square]))
    return combine([p[0] for p in parts], [p[1] for p in parts], rows)


def split(vector, pieces):
    out = []
    for _ in range(pieces):
        high = lax.reduce_precision(vector, 8, 7)
        out.append(high.astype(BF16))
        vector = vector - high
    return out


def extra_rows(vectors):
    rows = [piece for vector, pieces in vectors for piece in split(vector, pieces)]
    stacked = jnp.stack(rows)
    return jnp.pad(stacked, ((0, EXTRA - len(rows)),) + ((0, 0),) * (stacked.ndim - 1))


def read_rows(rows, pieces):
    out, at = [], 0
    for count in pieces:
        out.append(sum(rows[at + k] for k in range(count)))
        at += count
    return out


def local(view_one, view_two, proj_weight):
    rows, width = view_one.shape
    n_zl, n_y, n_x = lax.axis_size("zl"), lax.axis_size("y"), lax.axis_size("x")
    n_plane = n_y * n_x
    total_rows = rows * n_zl * n_plane
    blk_i, blk_j = width // n_x, width // n_y
    core = lax.axis_index("c")
    zh = lax.axis_index("zh")

    crossed = swap(view_two, "zh")
    send_one = view_one.reshape(rows, n_x, blk_i).transpose(1, 0, 2)
    send_one = jnp.broadcast_to(send_one[None], (n_y, n_x, rows, blk_i)).reshape(n_plane, rows, blk_i)
    own_one = lax.all_to_all(send_one, PLANE, 0, 0, tiled=True).reshape(n_plane * rows, blk_i)

    def two_blocks(own, other):
        return jnp.concatenate(
            [own.reshape(own.shape[0], n_y, blk_j), other.reshape(own.shape[0], n_y, blk_j)], axis=2
        ).transpose(1, 0, 2)

    stats_own = jnp.stack(moments(view_two))
    stats_all = two_blocks(stats_own, swap(stats_own, "zh"))
    both = jnp.concatenate(
        [
            two_blocks(view_two, crossed),
            extra_rows([(stats_all[:, 0], 3), (stats_all[:, 1], 3)]).transpose(1, 0, 2),
        ],
        axis=1,
    )
    slot_rows = rows + EXTRA
    both = jnp.broadcast_to(both[:, None], (n_y, n_x, slot_rows, 2 * blk_j))
    both = lax.all_to_all(
        both.reshape(n_plane, slot_rows, 2 * blk_j), PLANE, 0, 0, tiled=True
    )
    plane_two = both[:, :rows].reshape(n_plane * rows, 2 * blk_j)
    group_mean, group_square = read_rows(both[:, rows:].astype(F32).transpose(1, 0, 2), (3, 3))
    mean_two = jnp.mean(group_mean, axis=0)
    square_two = jnp.sum(group_square + rows * n_zl * (group_mean - mean_two) ** 2, axis=0)
    rstd_two = lax.rsqrt(square_two / total_rows + EPSILON)

    plane_one = jnp.concatenate([own_one, swap(own_one, "c")], axis=1)
    mean_one, square_one = moments(plane_one)
    rstd_one = lax.rsqrt(square_one / total_rows + EPSILON)
    norm_one = ((plane_one.astype(F32) - mean_one) * rstd_one).astype(BF16)
    norm_two = ((plane_two.astype(F32) - mean_two) * rstd_two).astype(BF16)

    tile_i, tile_j = norm_one.shape[1], norm_two.shape[1]
    part = dot(norm_one, norm_two, 0, 0).astype(BF16).reshape(n_zl, tile_i // n_zl, tile_j)
    sums = extra_rows(
        [(jnp.sum(norm_one.astype(F32), axis=0), 2), (jnp.sum(norm_two.astype(F32), axis=0), 2)]
    )
    part = jnp.concatenate([part, jnp.broadcast_to(sums[None], (n_zl,) + sums.shape)], axis=1)
    part = jnp.sum(lax.all_to_all(part, "zl", 0, 0, tiled=True).astype(F32), axis=0)
    slice_i = tile_i // n_zl
    mu_one, mu_two = (v / total_rows for v in read_rows(part[slice_i:], (2, 2)))
    corr = part[:slice_i] / total_rows
    on_diag = lax.axis_index("x") == lax.axis_index("y")

    def diagonal(height, first):
        row_ids = first + lax.broadcasted_iota(jnp.int32, (height, tile_j), 0)
        col_ids = lax.broadcasted_iota(jnp.int32, (height, tile_j), 1)
        return (row_ids == col_ids) & (row_ids < blk_i) & on_diag

    grad = jnp.where(
        diagonal(slice_i, lax.axis_index("zl") * slice_i),
        -2.0 * (1.0 - corr),
        2.0 * OFF_WEIGHT * corr,
    ).astype(BF16)
    grad = gather_zl(grad).reshape(tile_i, tile_j)

    wide = grad.astype(F32)
    product = wide * jnp.where(diagonal(tile_i, 0), 1.0 + 0.5 * wide, wide / (2.0 * OFF_WEIGHT))
    cross_one, mean_up_one = jnp.sum(product, axis=1), jnp.sum(wide * mu_two[None, :], axis=1)
    cross_two, mean_up_two = jnp.sum(product, axis=0), jnp.sum(wide * mu_one[:, None], axis=0)

    def to_rows(upstream, vectors):
        columns = upstream.shape[1]
        extra = extra_rows(vectors)
        slots = upstream.astype(BF16).reshape(n_plane, rows, columns)
        return jnp.concatenate([slots, jnp.broadcast_to(extra[None], (n_plane,) + extra.shape)], axis=1)

    def exchange(slots):
        out = lax.all_to_all(slots, PLANE, 0, 0, tiled=True)
        return out.reshape(n_y, n_x, slot_rows, slots.shape[2]).astype(F32)

    def delta(view, upstream, cross, mean_up, mean, rstd):
        normal = ((view.astype(F32) - mean) * rstd).astype(BF16).astype(F32)
        return (rstd * (upstream - mean_up - normal * cross)).astype(BF16)

    pieces = (2, 2, 3, 3)
    slots_two = to_rows(
        dot(norm_one, grad, 1, 0),
        [(cross_two, 2), (mean_up_two, 2), (mean_two / n_x, 3), (rstd_two / n_x, 3)],
    )
    got_two = lax.all_to_all(slots_two, PLANE, 0, 0, tiled=True)

    up_one = dot(norm_two, grad, 1, 1)
    other = jnp.concatenate(
        [
            up_one[:, blk_i:].astype(BF16),
            extra_rows([(cross_one[blk_i:], 2), (mean_up_one[blk_i:], 2)]),
        ],
        axis=0,
    )
    other = swap(other, "c").astype(F32)
    plane_rows = n_plane * rows
    up_one = up_one[:, :blk_i] + other[:plane_rows]
    tail = read_rows(other[plane_rows:], (2, 2))
    slots_one = to_rows(
        up_one,
        [
            (cross_one[:blk_i] + tail[0], 2),
            (mean_up_one[:blk_i] + tail[1], 2),
            (mean_one[:blk_i] / n_y, 3),
            (rstd_one[:blk_i] / n_y, 3),
        ],
    )
    got_two, slots_one = lax.optimization_barrier((got_two, slots_one))
    got_one = lax.all_to_all(slots_one, PLANE, 0, 0, tiled=True)

    got_two = jnp.sum(
        got_two.reshape(n_y, n_x, slot_rows, 2 * blk_j).astype(F32), axis=1
    ).transpose(1, 0, 2)
    own_two, far_two = got_two[:, :, :blk_j].reshape(slot_rows, width), got_two[:, :, blk_j:].reshape(slot_rows, width)
    far_cross, far_mean = read_rows(far_two[rows:], (2, 2))
    sent = jnp.concatenate(
        [far_two[:rows].astype(BF16), extra_rows([(far_cross, 2), (far_mean, 2)])], axis=0
    )
    sent = swap(sent, "zh").astype(F32)
    cross_two, mean_up_two, mean_two, rstd_two = read_rows(own_two[rows:], pieces)
    far_cross, far_mean = read_rows(sent[rows:], (2, 2))
    delta_two = delta(
        view_two, own_two[:rows] + sent[:rows], cross_two + far_cross, mean_up_two + far_mean, mean_two, rstd_two
    )

    got_one = jnp.sum(got_one.reshape(n_y, n_x, slot_rows, blk_i).astype(F32), axis=0)
    got_one = got_one.transpose(1, 0, 2).reshape(slot_rows, width)
    delta_one = delta(view_one, got_one[:rows], *read_rows(got_one[rows:], pieces))

    weight = proj_weight.reshape(2, 2, width, width)

    def block(half, member):
        return lax.dynamic_slice(weight, (half, member, 0, 0), (1, 1, width, width)).reshape(width, width)

    far_give, far_keep = block(1 - zh, 1 - core), block(1 - zh, core)
    near_give, near_keep = block(zh, 1 - core), block(zh, core)

    def input_grad(value):
        far = dot(value, far_keep, 1, 1) + swap(dot(value, far_give, 1, 1).astype(BF16), "c").astype(F32)
        far = swap(far.astype(BF16), "zh").astype(F32)
        near = dot(value, near_keep, 1, 1) + swap(dot(value, near_give, 1, 1).astype(BF16), "c").astype(F32)
        return (near + far).astype(BF16)

    grad_two = input_grad(delta_two)
    return input_grad(delta_one), grad_two


def solution(mesh):
    fine = Mesh(mesh.devices.reshape(4, 4, 4, 2, 2), ("zl", "y", "x", "zh", "c"))
    spec = P(("zl", "y", "x"), ("zh", "c"))
    return jax.shard_map(
        local,
        mesh=fine,
        in_specs=(spec, spec, P(None, ("zh", "c"))),
        out_specs=(spec, spec),
        check_vma=False,
    )
```

```python
import jax
import jax.numpy as jnp
from jax import lax
from jax.sharding import Mesh, PartitionSpec as P

OFF_WEIGHT = 0.0125
EPSILON = 1e-05
F32 = jnp.float32
BF16 = jnp.bfloat16
PLANE = ("y", "x")
SWAP = [(0, 1), (1, 0)]
EXTRA = 16


def dot(left, right, left_dim, right_dim):
    return lax.dot_general(
        left, right, (((left_dim,), (right_dim,)), ((), ())), preferred_element_type=F32
    )


def swap(value, axis):
    return lax.ppermute(value, axis, SWAP)


def gather_zl(value):
    count = lax.axis_size("zl")
    return lax.all_to_all(
        jnp.broadcast_to(value[None], (count,) + value.shape), "zl", 0, 0, tiled=True
    )


def small_gather_zl(value):
    count = lax.axis_size("zl")
    parts = [value]
    for shift in range(1, count):
        parts.append(lax.ppermute(value, "zl", [(i, (i + shift) % count) for i in range(count)]))
    return parts


def combine(means, squares, rows):
    mean = sum(means) / len(means)
    return mean, sum(squares) + rows * sum((m - mean) ** 2 for m in means)


def moments(values):
    rows = values.shape[0]
    wide = values.astype(F32)
    mean = jnp.sum(wide, axis=0) / rows
    square = jnp.sum((wide - mean) ** 2, axis=0)
    parts = small_gather_zl(jnp.stack([mean, square]))
    return combine([p[0] for p in parts], [p[1] for p in parts], rows)


def split(vector, pieces):
    out = []
    for _ in range(pieces):
        high = lax.reduce_precision(vector, 8, 7)
        out.append(high.astype(BF16))
        vector = vector - high
    return out


def extra_rows(vectors):
    rows = [piece for vector, pieces in vectors for piece in split(vector, pieces)]
    stacked = jnp.stack(rows)
    return jnp.pad(stacked, ((0, EXTRA - len(rows)),) + ((0, 0),) * (stacked.ndim - 1))


def read_rows(rows, pieces):
    out, at = [], 0
    for count in pieces:
        out.append(sum(rows[at + k] for k in range(count)))
        at += count
    return out


def local(view_one, view_two, proj_weight):
    rows, width = view_one.shape
    n_zl, n_y, n_x = lax.axis_size("zl"), lax.axis_size("y"), lax.axis_size("x")
    n_plane = n_y * n_x
    total_rows = rows * n_zl * n_plane
    blk_i, blk_j = width // n_x, width // n_y
    core = lax.axis_index("c")
    zh = lax.axis_index("zh")

    def column_blocks(view, count):
        return view.reshape(rows, count, width // count).transpose(1, 0, 2)

    def to_plane(slots):
        slots = jnp.broadcast_to(slots, (n_y, n_x) + slots.shape[2:])
        out = lax.all_to_all(slots.reshape((n_plane,) + slots.shape[2:]), PLANE, 0, 0, tiled=True)
        return out.reshape(n_plane * rows, slots.shape[3])

    crossed = swap(view_two, "zh")
    own = to_plane(
        jnp.concatenate(
            [
                jnp.broadcast_to(column_blocks(view_one, n_x)[None], (n_y, n_x, rows, blk_i)),
                jnp.broadcast_to(column_blocks(view_two, n_y)[:, None], (n_y, n_x, rows, blk_j)),
            ],
            axis=3,
        )
    )
    crossed, own = lax.optimization_barrier((crossed, own))
    far_two = to_plane(column_blocks(crossed, n_y)[:, None])

    def normalize(values, mean, rstd):
        return ((values.astype(F32) - mean) * rstd).astype(BF16)

    mean, square = moments(own)
    rstd = lax.rsqrt(square / total_rows + EPSILON)
    far_stats = swap(jnp.stack([mean[blk_i:], rstd[blk_i:]]), "zh")
    norm_own = normalize(own, mean, rstd)
    sums_own = jnp.sum(norm_own.astype(F32), axis=0)
    sums_one = jnp.concatenate([sums_own[:blk_i], swap(sums_own[:blk_i], "c")])
    sums_two = jnp.concatenate([sums_own[blk_i:], swap(sums_own[blk_i:], "zh")])
    norm_one = jnp.concatenate([norm_own[:, :blk_i], swap(norm_own[:, :blk_i], "c")], axis=1)
    norm_two = jnp.concatenate([norm_own[:, blk_i:], normalize(far_two, far_stats[0], far_stats[1])], axis=1)
    mean_one, rstd_one, mean_two, rstd_two = mean[:blk_i], rstd[:blk_i], mean[blk_i:], rstd[blk_i:]

    tile_i, tile_j = norm_one.shape[1], norm_two.shape[1]
    part = dot(norm_one, norm_two, 0, 0).astype(BF16).reshape(n_zl, tile_i // n_zl, tile_j)
    sums = extra_rows([(sums_one, 2), (sums_two, 2)])
    part = jnp.concatenate([part, jnp.broadcast_to(sums[None], (n_zl,) + sums.shape)], axis=1)
    part = jnp.sum(lax.all_to_all(part, "zl", 0, 0, tiled=True).astype(F32), axis=0)
    slice_i = tile_i // n_zl
    mu_one, mu_two = (v / total_rows for v in read_rows(part[slice_i:], (2, 2)))
    corr = part[:slice_i] / total_rows
    on_diag = lax.axis_index("x") == lax.axis_index("y")

    def diagonal(height, first):
        row_ids = first + lax.broadcasted_iota(jnp.int32, (height, tile_j), 0)
        col_ids = lax.broadcasted_iota(jnp.int32, (height, tile_j), 1)
        return (row_ids == col_ids) & (row_ids < blk_i) & on_diag

    grad = jnp.where(
        diagonal(slice_i, lax.axis_index("zl") * slice_i),
        -2.0 * (1.0 - corr),
        2.0 * OFF_WEIGHT * corr,
    ).astype(BF16)
    grad = gather_zl(grad).reshape(tile_i, tile_j)

    def products(grad):
        wide = grad.astype(F32)
        return wide, wide * jnp.where(diagonal(tile_i, 0), 1.0 + 0.5 * wide, wide / (2.0 * OFF_WEIGHT))

    def to_rows(upstream, vectors):
        columns = upstream.shape[1]
        extra = extra_rows(vectors)
        slots = upstream.astype(BF16).reshape(n_plane, rows, columns)
        return jnp.concatenate([slots, jnp.broadcast_to(extra[None], (n_plane,) + extra.shape)], axis=1)

    def delta(view, upstream, cross, mean_up, mean, rstd):
        normal = ((view.astype(F32) - mean) * rstd).astype(BF16).astype(F32)
        return (rstd * (upstream - mean_up - normal * cross)).astype(BF16)

    pieces = (2, 2, 3, 3)
    slot_rows = rows + EXTRA
    wide, product = products(grad)
    slots_two = to_rows(
        dot(norm_one, grad, 1, 0),
        [
            (jnp.sum(product, axis=0), 2),
            (jnp.sum(wide * mu_one[:, None], axis=0), 2),
            (jnp.pad(mean_two, (0, blk_j)) / n_x, 3),
            (jnp.pad(rstd_two, (0, blk_j)) / n_x, 3),
        ],
    )
    slots_two, grad = lax.optimization_barrier((slots_two, grad))
    got_two = lax.all_to_all(slots_two, PLANE, 0, 0, tiled=True)

    wide, product = products(grad)
    cross_one, mean_up_one = jnp.sum(product, axis=1), jnp.sum(wide * mu_two[None, :], axis=1)
    up_one = dot(norm_two, grad, 1, 1)
    other = jnp.concatenate(
        [
            up_one[:, blk_i:].astype(BF16),
            extra_rows([(cross_one[blk_i:], 2), (mean_up_one[blk_i:], 2)]),
        ],
        axis=0,
    )
    other = swap(other, "c").astype(F32)
    plane_rows = n_plane * rows
    up_one = up_one[:, :blk_i] + other[:plane_rows]
    tail = read_rows(other[plane_rows:], (2, 2))
    slots_one = to_rows(
        up_one,
        [
            (cross_one[:blk_i] + tail[0], 2),
            (mean_up_one[:blk_i] + tail[1], 2),
            (mean_one / n_y, 3),
            (rstd_one / n_y, 3),
        ],
    )
    got_two, slots_one = lax.optimization_barrier((got_two, slots_one))
    got_one = lax.all_to_all(slots_one, PLANE, 0, 0, tiled=True)

    got_two = jnp.sum(
        got_two.reshape(n_y, n_x, slot_rows, 2 * blk_j).astype(F32), axis=1
    ).transpose(1, 0, 2)
    own_two, far_two = got_two[:, :, :blk_j].reshape(slot_rows, width), got_two[:, :, blk_j:].reshape(slot_rows, width)
    far_cross, far_mean = read_rows(far_two[rows:], (2, 2))
    sent = jnp.concatenate(
        [far_two[:rows].astype(BF16), extra_rows([(far_cross, 2), (far_mean, 2)])], axis=0
    )
    sent = swap(sent, "zh").astype(F32)
    cross_two, mean_up_two, mean_two, rstd_two = read_rows(own_two[rows:], pieces)
    far_cross, far_mean = read_rows(sent[rows:], (2, 2))
    delta_two = delta(
        view_two, own_two[:rows] + sent[:rows], cross_two + far_cross, mean_up_two + far_mean, mean_two, rstd_two
    )

    got_one = jnp.sum(got_one.reshape(n_y, n_x, slot_rows, blk_i).astype(F32), axis=0)
    got_one = got_one.transpose(1, 0, 2).reshape(slot_rows, width)
    delta_one = delta(view_one, got_one[:rows], *read_rows(got_one[rows:], pieces))

    weight = proj_weight.reshape(2, 2, width, width)

    def block(half, member):
        return lax.dynamic_slice(weight, (half, member, 0, 0), (1, 1, width, width)).reshape(width, width)

    far_give, far_keep = block(1 - zh, 1 - core), block(1 - zh, core)
    near_give, near_keep = block(zh, 1 - core), block(zh, core)

    def input_grad(value):
        far = dot(value, far_keep, 1, 1) + swap(dot(value, far_give, 1, 1).astype(BF16), "c").astype(F32)
        far = swap(far.astype(BF16), "zh").astype(F32)
        near = dot(value, near_keep, 1, 1) + swap(dot(value, near_give, 1, 1).astype(BF16), "c").astype(F32)
        return (near + far).astype(BF16)

    grad_two = input_grad(delta_two)
    return input_grad(delta_one), grad_two


def solution(mesh):
    fine = Mesh(mesh.devices.reshape(4, 4, 4, 2, 2), ("zl", "y", "x", "zh", "c"))
    spec = P(("zl", "y", "x"), ("zh", "c"))
    return jax.shard_map(
        local,
        mesh=fine,
        in_specs=(spec, spec, P(None, ("zh", "c"))),
        out_specs=(spec, spec),
        check_vma=False,
    )
```

```python
import jax
import jax.numpy as jnp
from jax import lax
from jax.sharding import Mesh, PartitionSpec as P

OFF_WEIGHT = 0.0125
EPSILON = 1e-05
F32 = jnp.float32
BF16 = jnp.bfloat16
SWAP = [(0, 1), (1, 0)]
EXTRA = 16


def dot(left, right, left_dim, right_dim):
    return lax.dot_general(
        left, right, (((left_dim,), (right_dim,)), ((), ())), preferred_element_type=F32
    )


def swap(value, axis):
    return lax.ppermute(value, axis, SWAP)


def gather_zl(value):
    count = lax.axis_size("zl")
    return lax.all_to_all(
        jnp.broadcast_to(value[None], (count,) + value.shape), "zl", 0, 0, tiled=True
    )


def shift(value, axis, step):
    count = lax.axis_size(axis)
    return lax.ppermute(value, axis, [(i, (i + step) % count) for i in range(count)])


def small_gather_zl(value):
    return [value] + [shift(value, "zl", step) for step in range(1, lax.axis_size("zl"))]


def rotate(value, start):
    return lax.dynamic_slice_in_dim(jnp.concatenate([value, value], axis=1), start, value.shape[1], 1)


def scatter_columns(rotated, axis):
    count = lax.axis_size(axis)
    blocks = jnp.split(rotated, count, axis=1)
    return jnp.concatenate([blocks[0]] + [shift(blocks[k], axis, k) for k in range(1, count)], axis=0)


def gather_columns(stacked, axis):
    count = lax.axis_size(axis)
    blocks = jnp.split(stacked, count, axis=0)
    return jnp.concatenate([blocks[0]] + [shift(blocks[k], axis, -k) for k in range(1, count)], axis=1)


def spread(value, axis):
    return [value] + [shift(value, axis, k) for k in range(1, lax.axis_size(axis))]


def collect(pieces, axis):
    return sum(
        (piece if k == 0 else shift(piece, axis, -k)).astype(F32) for k, piece in enumerate(pieces)
    )


def combine(means, squares, rows):
    mean = sum(means) / len(means)
    return mean, sum(squares) + rows * sum((m - mean) ** 2 for m in means)


def moments(values):
    rows = values.shape[0]
    wide = values.astype(F32)
    mean = jnp.sum(wide, axis=0) / rows
    square = jnp.sum((wide - mean) ** 2, axis=0)
    parts = small_gather_zl(jnp.stack([mean, square]))
    return combine([p[0] for p in parts], [p[1] for p in parts], rows)


def split(vector, pieces):
    out = []
    for _ in range(pieces):
        high = lax.reduce_precision(vector, 8, 7)
        out.append(high.astype(BF16))
        vector = vector - high
    return out


def extra_rows(vectors):
    rows = [piece for vector, pieces in vectors for piece in split(vector, pieces)]
    stacked = jnp.stack(rows)
    return jnp.pad(stacked, ((0, EXTRA - len(rows)),) + ((0, 0),) * (stacked.ndim - 1))


def read_rows(rows, pieces):
    out, at = [], 0
    for count in pieces:
        out.append(sum(rows[at + k] for k in range(count)))
        at += count
    return out


def local(view_one, view_two, proj_weight):
    rows, width = view_one.shape
    n_zl, n_y, n_x = lax.axis_size("zl"), lax.axis_size("y"), lax.axis_size("x")
    n_plane = n_y * n_x
    total_rows = rows * n_zl * n_plane
    blk_i, blk_j = width // n_x, width // n_y
    core = lax.axis_index("c")
    zh = lax.axis_index("zh")

    at_x, at_y = lax.axis_index("x"), lax.axis_index("y")
    rotated_two = rotate(view_two, at_y * blk_j)
    crossed = swap(rotated_two, "zh")
    rotated_one = rotate(view_one, at_x * blk_i)
    plane_rows = n_plane * rows

    def plane_of_two(rotated):
        parts = spread(scatter_columns(rotated, "y"), "x")
        parts = [part.reshape(n_y, 1, rows, blk_j) for part in parts]
        return jnp.concatenate(parts, axis=1).reshape(plane_rows, blk_j)

    own_one = jnp.concatenate(spread(scatter_columns(rotated_one, "x"), "y"), axis=0)
    own = jnp.concatenate([own_one, plane_of_two(rotated_two)], axis=1)
    far_two = plane_of_two(crossed)

    def normalize(values, mean, rstd):
        return ((values.astype(F32) - mean) * rstd).astype(BF16)

    mean, square = moments(own)
    rstd = lax.rsqrt(square / total_rows + EPSILON)
    far_stats = swap(jnp.stack([mean[blk_i:], rstd[blk_i:]]), "zh")
    norm_own = normalize(own, mean, rstd)
    sums_own = jnp.sum(norm_own.astype(F32), axis=0)
    sums_one = jnp.concatenate([sums_own[:blk_i], swap(sums_own[:blk_i], "c")])
    sums_two = jnp.concatenate([sums_own[blk_i:], swap(sums_own[blk_i:], "zh")])
    norm_one = jnp.concatenate([norm_own[:, :blk_i], swap(norm_own[:, :blk_i], "c")], axis=1)
    norm_two = jnp.concatenate([norm_own[:, blk_i:], normalize(far_two, far_stats[0], far_stats[1])], axis=1)
    rstd_one, rstd_two = rstd[:blk_i], rstd[blk_i:]

    tile_i, tile_j = norm_one.shape[1], norm_two.shape[1]
    part = dot(norm_one, norm_two, 0, 0).astype(BF16).reshape(n_zl, tile_i // n_zl, tile_j)
    sums = extra_rows([(sums_one, 2), (sums_two, 2)])
    part = jnp.concatenate([part, jnp.broadcast_to(sums[None], (n_zl,) + sums.shape)], axis=1)
    part = jnp.sum(lax.all_to_all(part, "zl", 0, 0, tiled=True).astype(F32), axis=0)
    slice_i = tile_i // n_zl
    mu_one, mu_two = (v / total_rows for v in read_rows(part[slice_i:], (2, 2)))
    corr = part[:slice_i] / total_rows
    on_diag = lax.axis_index("x") == lax.axis_index("y")

    def diagonal(height, first):
        row_ids = first + lax.broadcasted_iota(jnp.int32, (height, tile_j), 0)
        col_ids = lax.broadcasted_iota(jnp.int32, (height, tile_j), 1)
        return (row_ids == col_ids) & (row_ids < blk_i) & on_diag

    grad = jnp.where(
        diagonal(slice_i, lax.axis_index("zl") * slice_i),
        -2.0 * (1.0 - corr),
        2.0 * OFF_WEIGHT * corr,
    ).astype(BF16)
    grad = gather_zl(grad).reshape(tile_i, tile_j)

    def products(grad):
        wide = grad.astype(F32)
        return wide, wide * jnp.where(diagonal(tile_i, 0), 1.0 + 0.5 * wide, wide / (2.0 * OFF_WEIGHT))

    def delta(normal, upstream, cross, mean_up, rstd):
        return (rstd * (upstream - mean_up - normal.astype(F32) * cross)).astype(BF16)

    def with_extra(piece, extra):
        return jnp.concatenate([piece.reshape(-1, piece.shape[-1]), extra], axis=0)

    wide, product = products(grad)
    cross_two, mean_up_two = jnp.sum(product, axis=0), jnp.sum(wide * mu_one[:, None], axis=0)
    up_two = dot(norm_one, grad, 1, 0).astype(BF16).reshape(n_y, n_x, rows, tile_j)

    def along_x(columns):
        extra = extra_rows([(cross_two[columns], 2), (mean_up_two[columns], 2)])
        return collect([with_extra(up_two[:, k, :, columns], extra) for k in range(n_x)], "x")

    part_rows = n_y * rows
    far = along_x(slice(blk_j, None))
    far = with_extra(
        far[:part_rows].astype(BF16), extra_rows([(v, 2) for v in read_rows(far[part_rows:], (2, 2))])
    )
    far = swap(far, "zh").astype(F32)

    wide, product = products(grad)
    cross_one, mean_up_one = jnp.sum(product, axis=1), jnp.sum(wide * mu_two[None, :], axis=1)
    up_one = dot(norm_two, grad, 1, 1)
    other = with_extra(
        up_one[:, blk_i:].astype(BF16), extra_rows([(cross_one[blk_i:], 2), (mean_up_one[blk_i:], 2)])
    )
    other = swap(other, "c").astype(F32)
    up_one = (up_one[:, :blk_i] + other[:plane_rows]).astype(BF16).reshape(n_y, n_x * rows, blk_i)
    tail = read_rows(other[plane_rows:], (2, 2))
    extra = extra_rows([(cross_one[:blk_i] + tail[0], 2), (mean_up_one[:blk_i] + tail[1], 2)])
    up_one = collect([with_extra(up_one[k], extra) for k in range(n_y)], "y")
    cross_one, mean_up_one = read_rows(up_one[n_x * rows :], (2, 2))
    delta_one = delta(
        norm_one[: n_x * rows, :blk_i], up_one[: n_x * rows], cross_one, mean_up_one, rstd_one
    )
    delta_one = rotate(gather_columns(delta_one, "x"), ((n_x - at_x) % n_x) * blk_i)

    near = along_x(slice(0, blk_j))
    up_two = near[:part_rows] + far[:part_rows]
    cross_two, mean_up_two = (
        a + b for a, b in zip(read_rows(near[part_rows:], (2, 2)), read_rows(far[part_rows:], (2, 2)))
    )
    normal = norm_two.reshape(n_y, n_x, rows, tile_j)[:, 0, :, :blk_j].reshape(part_rows, blk_j)
    delta_two = delta(normal, up_two, cross_two, mean_up_two, rstd_two)
    delta_two = rotate(gather_columns(delta_two, "y"), ((n_y - at_y) % n_y) * blk_j)

    weight = proj_weight.reshape(2, 2, width, width)

    def block(half, member):
        return lax.dynamic_slice(weight, (half, member, 0, 0), (1, 1, width, width)).reshape(width, width)

    far_give, far_keep = block(1 - zh, 1 - core), block(1 - zh, core)
    near_give, near_keep = block(zh, 1 - core), block(zh, core)

    def input_grad(value):
        far = dot(value, far_keep, 1, 1) + swap(dot(value, far_give, 1, 1).astype(BF16), "c").astype(F32)
        far = swap(far.astype(BF16), "zh").astype(F32)
        near = dot(value, near_keep, 1, 1) + swap(dot(value, near_give, 1, 1).astype(BF16), "c").astype(F32)
        return (near + far).astype(BF16)

    grad_two = input_grad(delta_two)
    return input_grad(delta_one), grad_two


def solution(mesh):
    fine = Mesh(mesh.devices.reshape(4, 4, 4, 2, 2), ("zl", "y", "x", "zh", "c"))
    spec = P(("zl", "y", "x"), ("zh", "c"))
    return jax.shard_map(
        local,
        mesh=fine,
        in_specs=(spec, spec, P(None, ("zh", "c"))),
        out_specs=(spec, spec),
        check_vma=False,
    )
```

```python
import jax
import jax.numpy as jnp
from jax import lax
from jax.sharding import Mesh, PartitionSpec as P

OFF_WEIGHT = 0.0125
EPSILON = 1e-05
F32 = jnp.float32
BF16 = jnp.bfloat16
SWAP = [(0, 1), (1, 0)]
EXTRA = 16


def dot(left, right, left_dim, right_dim):
    return lax.dot_general(
        left, right, (((left_dim,), (right_dim,)), ((), ())), preferred_element_type=F32
    )


def swap(value, axis):
    return lax.ppermute(value, axis, SWAP)


def gather_zl(value):
    count = lax.axis_size("zl")
    return lax.all_to_all(
        jnp.broadcast_to(value[None], (count,) + value.shape), "zl", 0, 0, tiled=True
    )


def shift(value, axis, step):
    count = lax.axis_size(axis)
    return lax.ppermute(value, axis, [(i, (i + step) % count) for i in range(count)])


def small_gather_zl(value):
    return [value] + [shift(value, "zl", step) for step in range(1, lax.axis_size("zl"))]


def rotate(value, start):
    return lax.dynamic_slice_in_dim(jnp.concatenate([value, value], axis=1), start, value.shape[1], 1)


def scatter_columns(rotated, axis):
    count = lax.axis_size(axis)
    blocks = jnp.split(rotated, count, axis=1)
    return jnp.concatenate([blocks[0]] + [shift(blocks[k], axis, k) for k in range(1, count)], axis=0)


def gather_columns(blocks, axis):
    return jnp.concatenate([blocks[0]] + [shift(blocks[k], axis, -k) for k in range(1, len(blocks))], axis=1)


def spread(value, axis):
    return [value] + [shift(value, axis, k) for k in range(1, lax.axis_size(axis))]


def collect(pieces, axis):
    return sum(
        (piece if k == 0 else shift(piece, axis, -k)).astype(F32) for k, piece in enumerate(pieces)
    )


def trade(slots, axis):
    return lax.all_to_all(slots, axis, 0, 0, tiled=True)


def combine(means, squares, rows):
    mean = sum(means) / len(means)
    return mean, sum(squares) + rows * sum((m - mean) ** 2 for m in means)


def moments(values):
    rows = values.shape[0]
    wide = values.astype(F32)
    mean = jnp.sum(wide, axis=0) / rows
    square = jnp.sum((wide - mean) ** 2, axis=0)
    parts = small_gather_zl(jnp.stack([mean, square]))
    return combine([p[0] for p in parts], [p[1] for p in parts], rows)


def split(vector, pieces):
    out = []
    for _ in range(pieces):
        high = lax.reduce_precision(vector, 8, 7)
        out.append(high.astype(BF16))
        vector = vector - high
    return out


def extra_rows(vectors):
    rows = [piece for vector, pieces in vectors for piece in split(vector, pieces)]
    stacked = jnp.stack(rows)
    return jnp.pad(stacked, ((0, EXTRA - len(rows)),) + ((0, 0),) * (stacked.ndim - 1))


def read_rows(rows, pieces):
    out, at = [], 0
    for count in pieces:
        out.append(sum(rows[at + k] for k in range(count)))
        at += count
    return out


def local(view_one, view_two, proj_weight):
    rows, width = view_one.shape
    n_zl, n_y, n_x = lax.axis_size("zl"), lax.axis_size("y"), lax.axis_size("x")
    n_plane = n_y * n_x
    total_rows = rows * n_zl * n_plane
    blk_i, blk_j = width // n_x, width // n_y
    core = lax.axis_index("c")
    zh = lax.axis_index("zh")

    at_x, at_y = lax.axis_index("x"), lax.axis_index("y")
    rotated_two = rotate(view_two, at_y * blk_j)
    crossed = swap(rotated_two, "zh")
    plane_rows = n_plane * rows
    part_rows = n_y * rows

    def plane_of_two(rotated):
        part = scatter_columns(rotated, "y")
        return trade(jnp.broadcast_to(part[None], (n_x, part_rows, blk_j)), "x").reshape(plane_rows, blk_j)

    part_one = trade(view_one.reshape(rows, n_x, blk_i).transpose(1, 0, 2), "x")
    own_one = jnp.concatenate([part[:, None] for part in spread(part_one, "y")], axis=1)
    own = jnp.concatenate([own_one.reshape(plane_rows, blk_i), plane_of_two(rotated_two)], axis=1)
    far_two = plane_of_two(crossed)

    def normalize(values, mean, rstd):
        return ((values.astype(F32) - mean) * rstd).astype(BF16)

    mean, square = moments(own)
    rstd = lax.rsqrt(square / total_rows + EPSILON)
    norm_own = normalize(own, mean, rstd)
    sums_own = jnp.sum(norm_own.astype(F32), axis=0)
    far_stats = swap(jnp.stack([mean[blk_i:], rstd[blk_i:], sums_own[blk_i:]]), "zh")
    sums_one = jnp.concatenate([sums_own[:blk_i], swap(sums_own[:blk_i], "c")])
    sums_two = jnp.concatenate([sums_own[blk_i:], far_stats[2]])
    norm_one = jnp.concatenate([norm_own[:, :blk_i], swap(norm_own[:, :blk_i], "c")], axis=1)
    norm_two = jnp.concatenate([norm_own[:, blk_i:], normalize(far_two, far_stats[0], far_stats[1])], axis=1)
    rstd_one, rstd_two = rstd[:blk_i], rstd[blk_i:]

    tile_i, tile_j = norm_one.shape[1], norm_two.shape[1]
    part = dot(norm_one, norm_two, 0, 0).astype(BF16).reshape(n_zl, tile_i // n_zl, tile_j)
    sums = extra_rows([(sums_one, 2), (sums_two, 2)])
    part = jnp.concatenate([part, jnp.broadcast_to(sums[None], (n_zl,) + sums.shape)], axis=1)
    part = jnp.sum(lax.all_to_all(part, "zl", 0, 0, tiled=True).astype(F32), axis=0)
    slice_i = tile_i // n_zl
    mu_one, mu_two = (v / total_rows for v in read_rows(part[slice_i:], (2, 2)))
    corr = part[:slice_i] / total_rows
    on_diag = lax.axis_index("x") == lax.axis_index("y")

    def diagonal(height, first):
        row_ids = first + lax.broadcasted_iota(jnp.int32, (height, tile_j), 0)
        col_ids = lax.broadcasted_iota(jnp.int32, (height, tile_j), 1)
        return (row_ids == col_ids) & (row_ids < blk_i) & on_diag

    grad = jnp.where(
        diagonal(slice_i, lax.axis_index("zl") * slice_i),
        -2.0 * (1.0 - corr),
        2.0 * OFF_WEIGHT * corr,
    ).astype(BF16)
    grad = gather_zl(grad).reshape(tile_i, tile_j)

    def products(grad):
        wide = grad.astype(F32)
        return wide, wide * jnp.where(diagonal(tile_i, 0), 1.0 + 0.5 * wide, wide / (2.0 * OFF_WEIGHT))

    def delta(normal, upstream, cross, mean_up, rstd):
        return (rstd * (upstream - mean_up - normal.astype(F32) * cross)).astype(BF16)

    def with_extra(piece, extra):
        return jnp.concatenate([piece.reshape(-1, piece.shape[-1]), extra], axis=0)

    wide, product = products(grad)
    cross_two, mean_up_two = jnp.sum(product, axis=0), jnp.sum(wide * mu_one[:, None], axis=0)
    up_two = dot(norm_one, grad, 1, 0).astype(BF16).reshape(n_x, part_rows, tile_j)

    def for_x(columns):
        extra = extra_rows([(cross_two[columns], 2), (mean_up_two[columns], 2)])
        return jnp.concatenate(
            [up_two[:, :, columns], jnp.broadcast_to(extra[None], (n_x,) + extra.shape)], axis=1
        )

    slots_far, slots_near = for_x(slice(blk_j, None)), for_x(slice(0, blk_j))
    slots_far, slots_near, grad = lax.optimization_barrier((slots_far, slots_near, grad))

    far = jnp.sum(trade(slots_far, "x").astype(F32), axis=0)
    far = with_extra(
        far[:part_rows].astype(BF16), extra_rows([(v, 2) for v in read_rows(far[part_rows:], (2, 2))])
    )
    far = swap(far, "zh").astype(F32)

    wide, product = products(grad)
    cross_one, mean_up_one = jnp.sum(product, axis=1), jnp.sum(wide * mu_two[None, :], axis=1)
    up_one = dot(norm_two, grad, 1, 1)
    other = with_extra(
        up_one[:, blk_i:].astype(BF16), extra_rows([(cross_one[blk_i:], 2), (mean_up_one[blk_i:], 2)])
    )
    other = swap(other, "c").astype(F32)
    up_one = (up_one[:, :blk_i] + other[:plane_rows]).astype(BF16).reshape(n_x, n_y, rows, blk_i)
    tail = read_rows(other[plane_rows:], (2, 2))
    extra = extra_rows([(cross_one[:blk_i] + tail[0], 2), (mean_up_one[:blk_i] + tail[1], 2)])
    up_one = collect([with_extra(up_one[:, k], extra) for k in range(n_y)], "y")
    cross_one, mean_up_one = read_rows(up_one[n_x * rows :], (2, 2))
    normal = norm_one.reshape(n_x, n_y, rows, tile_i)[:, 0, :, :blk_i].reshape(n_x * rows, blk_i)
    delta_one = delta(normal, up_one[: n_x * rows], cross_one, mean_up_one, rstd_one)
    delta_one = [
        lax.dynamic_slice_in_dim(delta_one, (at_x + n_x - k) % n_x * rows, rows, 0) for k in range(n_x)
    ]
    delta_one = rotate(gather_columns(delta_one, "x"), ((n_x - at_x) % n_x) * blk_i)

    near = jnp.sum(trade(slots_near, "x").astype(F32), axis=0)
    up_two = near[:part_rows] + far[:part_rows]
    cross_two, mean_up_two = (
        a + b for a, b in zip(read_rows(near[part_rows:], (2, 2)), read_rows(far[part_rows:], (2, 2)))
    )
    normal = lax.dynamic_slice(norm_two, (at_x * part_rows, 0), (part_rows, blk_j))
    delta_two = delta(normal, up_two, cross_two, mean_up_two, rstd_two)
    delta_two = gather_columns(jnp.split(delta_two, n_y, axis=0), "y")
    delta_two = rotate(delta_two, ((n_y - at_y) % n_y) * blk_j)

    weight = proj_weight.reshape(2, 2, width, width)

    def block(half, member):
        return lax.dynamic_slice(weight, (half, member, 0, 0), (1, 1, width, width)).reshape(width, width)

    far_give, far_keep = block(1 - zh, 1 - core), block(1 - zh, core)
    near_give, near_keep = block(zh, 1 - core), block(zh, core)

    def input_grad(value):
        far = dot(value, far_keep, 1, 1) + swap(dot(value, far_give, 1, 1).astype(BF16), "c").astype(F32)
        far = swap(far.astype(BF16), "zh").astype(F32)
        near = dot(value, near_keep, 1, 1) + swap(dot(value, near_give, 1, 1).astype(BF16), "c").astype(F32)
        return (near + far).astype(BF16)

    grad_two = input_grad(delta_two)
    return input_grad(delta_one), grad_two


def solution(mesh):
    fine = Mesh(mesh.devices.reshape(4, 4, 4, 2, 2), ("zl", "y", "x", "zh", "c"))
    spec = P(("zl", "y", "x"), ("zh", "c"))
    return jax.shard_map(
        local,
        mesh=fine,
        in_specs=(spec, spec, P(None, ("zh", "c"))),
        out_specs=(spec, spec),
        check_vma=False,
    )
```

```python
import jax
import jax.numpy as jnp
from jax import lax
from jax.sharding import Mesh, PartitionSpec as P

OFF_WEIGHT = 0.0125
EPSILON = 1e-05
F32 = jnp.float32
BF16 = jnp.bfloat16
SWAP = [(0, 1), (1, 0)]
EXTRA = 16


def dot(left, right, left_dim, right_dim):
    return lax.dot_general(
        left, right, (((left_dim,), (right_dim,)), ((), ())), preferred_element_type=F32
    )


def swap(value, axis):
    return lax.ppermute(value, axis, SWAP)


def gather_zl(value):
    count = lax.axis_size("zl")
    return lax.all_to_all(
        jnp.broadcast_to(value[None], (count,) + value.shape), "zl", 0, 0, tiled=True
    )


def shift(value, axis, step):
    count = lax.axis_size(axis)
    return lax.ppermute(value, axis, [(i, (i + step) % count) for i in range(count)])


def small_gather_zl(value):
    return [value] + [shift(value, "zl", step) for step in range(1, lax.axis_size("zl"))]


def rotate(value, start, dim):
    doubled = jnp.concatenate([value, value], axis=dim)
    return lax.dynamic_slice_in_dim(doubled, start, value.shape[dim], dim)


def scatter_blocks(value, axis):
    return [value[0]] + [shift(value[k], axis, k) for k in range(1, len(value))]


def spread(value, axis):
    return [value] + [shift(value, axis, k) for k in range(1, lax.axis_size(axis))]


def collect(pieces, axis):
    return sum(
        (piece if k == 0 else shift(piece, axis, -k)).astype(F32) for k, piece in enumerate(pieces)
    )


def trade(slots, axis):
    return lax.all_to_all(slots, axis, 0, 0, tiled=True)


def combine(means, squares, rows):
    mean = sum(means) / len(means)
    return mean, sum(squares) + rows * sum((m - mean) ** 2 for m in means)


def moments(values):
    rows = values.shape[0]
    wide = values.astype(F32)
    mean = jnp.sum(wide, axis=0) / rows
    square = jnp.sum((wide - mean) ** 2, axis=0)
    parts = small_gather_zl(jnp.stack([mean, square]))
    return combine([p[0] for p in parts], [p[1] for p in parts], rows)


def split(vector, pieces):
    out = []
    for _ in range(pieces):
        high = lax.reduce_precision(vector, 8, 7)
        out.append(high.astype(BF16))
        vector = vector - high
    return out


def extra_rows(vectors):
    rows = [piece for vector, pieces in vectors for piece in split(vector, pieces)]
    stacked = jnp.stack(rows)
    return jnp.pad(stacked, ((0, EXTRA - len(rows)),) + ((0, 0),) * (stacked.ndim - 1))


def read_rows(rows, pieces):
    out, at = [], 0
    for count in pieces:
        out.append(sum(rows[at + k] for k in range(count)))
        at += count
    return out


def local(view_one, view_two, proj_weight):
    rows, width = view_one.shape
    n_zl, n_y, n_x = lax.axis_size("zl"), lax.axis_size("y"), lax.axis_size("x")
    n_plane = n_y * n_x
    total_rows = rows * n_zl * n_plane
    blk_i, blk_j = width // n_x, width // n_y
    core = lax.axis_index("c")
    zh = lax.axis_index("zh")

    at_x, at_y = lax.axis_index("x"), lax.axis_index("y")
    plane_rows = n_plane * rows
    part_rows = n_y * rows
    rotated_two = rotate(view_two, at_y * blk_j, 1)
    crossed = swap(rotated_two, "zh")
    rotated_one = rotate(view_one, at_x * blk_i, 1)
    part_one = jnp.concatenate(scatter_blocks(jnp.split(rotated_one, n_x, axis=1), "x"), axis=0)
    own_one = trade(jnp.broadcast_to(part_one[None], (n_y,) + part_one.shape), "y")

    def plane_of_two(rotated):
        parts = scatter_blocks(jnp.split(rotated, n_y, axis=1), "y")
        part = rotate(jnp.stack(parts[::-1]), n_y - 1 - at_y, 0)
        return jnp.concatenate([p[:, None] for p in spread(part, "x")], axis=1).reshape(plane_rows, blk_j)

    own = jnp.concatenate([own_one.reshape(plane_rows, blk_i), plane_of_two(rotated_two)], axis=1)
    far_two = plane_of_two(crossed)

    def normalize(values, mean, rstd):
        return ((values.astype(F32) - mean) * rstd).astype(BF16)

    mean, square = moments(own)
    rstd = lax.rsqrt(square / total_rows + EPSILON)
    norm_own = normalize(own, mean, rstd)
    sums_own = jnp.sum(norm_own.astype(F32), axis=0)
    far_stats = swap(jnp.stack([mean[blk_i:], rstd[blk_i:], sums_own[blk_i:]]), "zh")
    sums_one = jnp.concatenate([sums_own[:blk_i], swap(sums_own[:blk_i], "c")])
    sums_two = jnp.concatenate([sums_own[blk_i:], far_stats[2]])
    norm_one = jnp.concatenate([norm_own[:, :blk_i], swap(norm_own[:, :blk_i], "c")], axis=1)
    norm_two = jnp.concatenate([norm_own[:, blk_i:], normalize(far_two, far_stats[0], far_stats[1])], axis=1)
    rstd_one, rstd_two = rstd[:blk_i], rstd[blk_i:]

    tile_i, tile_j = norm_one.shape[1], norm_two.shape[1]
    part = dot(norm_one, norm_two, 0, 0).astype(BF16).reshape(n_zl, tile_i // n_zl, tile_j)
    sums = extra_rows([(sums_one, 2), (sums_two, 2)])
    part = jnp.concatenate([part, jnp.broadcast_to(sums[None], (n_zl,) + sums.shape)], axis=1)
    part = jnp.sum(lax.all_to_all(part, "zl", 0, 0, tiled=True).astype(F32), axis=0)
    slice_i = tile_i // n_zl
    mu_one, mu_two = (v / total_rows for v in read_rows(part[slice_i:], (2, 2)))
    corr = part[:slice_i] / total_rows
    on_diag = lax.axis_index("x") == lax.axis_index("y")

    def diagonal(height, first):
        row_ids = first + lax.broadcasted_iota(jnp.int32, (height, tile_j), 0)
        col_ids = lax.broadcasted_iota(jnp.int32, (height, tile_j), 1)
        return (row_ids == col_ids) & (row_ids < blk_i) & on_diag

    grad = jnp.where(
        diagonal(slice_i, lax.axis_index("zl") * slice_i),
        -2.0 * (1.0 - corr),
        2.0 * OFF_WEIGHT * corr,
    ).astype(BF16)
    grad = gather_zl(grad).reshape(tile_i, tile_j)

    def products(grad):
        wide = grad.astype(F32)
        return wide, wide * jnp.where(diagonal(tile_i, 0), 1.0 + 0.5 * wide, wide / (2.0 * OFF_WEIGHT))

    def delta(normal, upstream, cross, mean_up, rstd):
        return (rstd * (upstream - mean_up - normal.astype(F32) * cross)).astype(BF16)

    def with_extra(piece, extra):
        return jnp.concatenate([piece.reshape(-1, piece.shape[-1]), extra], axis=0)

    wide, product = products(grad)
    cross_two, mean_up_two = jnp.sum(product, axis=0), jnp.sum(wide * mu_one[:, None], axis=0)
    up_two = dot(norm_one, grad, 1, 0).astype(BF16).reshape(n_y, n_x, rows, tile_j)

    def for_x(columns):
        extra = extra_rows([(cross_two[columns], 2), (mean_up_two[columns], 2)])
        return [with_extra(up_two[:, k, :, columns], extra) for k in range(n_x)]

    pieces_far, pieces_near = for_x(slice(blk_j, None)), for_x(slice(0, blk_j))
    pieces_far, pieces_near, grad = lax.optimization_barrier((pieces_far, pieces_near, grad))

    far = collect(pieces_far, "x")
    far = with_extra(
        far[:part_rows].astype(BF16), extra_rows([(v, 2) for v in read_rows(far[part_rows:], (2, 2))])
    )
    far, pieces_near = lax.optimization_barrier((far, pieces_near))
    far = swap(far, "zh").astype(F32)

    wide, product = products(grad)
    cross_one, mean_up_one = jnp.sum(product, axis=1), jnp.sum(wide * mu_two[None, :], axis=1)
    up_one = dot(norm_two, grad, 1, 1)
    other = with_extra(
        up_one[:, blk_i:].astype(BF16), extra_rows([(cross_one[blk_i:], 2), (mean_up_one[blk_i:], 2)])
    )
    other = swap(other, "c").astype(F32)
    up_one = (up_one[:, :blk_i] + other[:plane_rows]).astype(BF16).reshape(n_y, n_x * rows, blk_i)
    tail = read_rows(other[plane_rows:], (2, 2))
    extra = extra_rows([(cross_one[:blk_i] + tail[0], 2), (mean_up_one[:blk_i] + tail[1], 2)])
    slots_one = jnp.concatenate([up_one, jnp.broadcast_to(extra[None], (n_y,) + extra.shape)], axis=1)
    up_one = jnp.sum(trade(slots_one, "y").astype(F32), axis=0)
    cross_one, mean_up_one = read_rows(up_one[n_x * rows :], (2, 2))
    normal = lax.dynamic_slice(norm_one, (at_y * n_x * rows, 0), (n_x * rows, blk_i))
    delta_one = delta(normal, up_one[: n_x * rows], cross_one, mean_up_one, rstd_one)
    back = scatter_blocks(jnp.split(delta_one, n_x, axis=0)[:1] + jnp.split(delta_one, n_x, axis=0)[:0:-1], "x")
    delta_one = rotate(jnp.concatenate(back[:1] + back[:0:-1], axis=1), (n_x - at_x) % n_x * blk_i, 1)

    near = collect(pieces_near, "x")
    up_two = near[:part_rows] + far[:part_rows]
    cross_two, mean_up_two = (
        a + b for a, b in zip(read_rows(near[part_rows:], (2, 2)), read_rows(far[part_rows:], (2, 2)))
    )
    normal = norm_two.reshape(n_y, n_x, rows, tile_j)[:, 0, :, :blk_j].reshape(part_rows, blk_j)
    delta_two = delta(normal, up_two, cross_two, mean_up_two, rstd_two)
    back = scatter_blocks(rotate(delta_two.reshape(n_y, rows, blk_j), at_y, 0), "y")
    delta_two = rotate(jnp.concatenate(back[:1] + back[:0:-1], axis=1), (n_y - at_y) % n_y * blk_j, 1)

    weight = proj_weight.reshape(2, 2, width, width)

    def block(half, member):
        return lax.dynamic_slice(weight, (half, member, 0, 0), (1, 1, width, width)).reshape(width, width)

    far_give, far_keep = block(1 - zh, 1 - core), block(1 - zh, core)
    near_give, near_keep = block(zh, 1 - core), block(zh, core)

    def input_grad(value):
        far = dot(value, far_keep, 1, 1) + swap(dot(value, far_give, 1, 1).astype(BF16), "c").astype(F32)
        far = swap(far.astype(BF16), "zh").astype(F32)
        near = dot(value, near_keep, 1, 1) + swap(dot(value, near_give, 1, 1).astype(BF16), "c").astype(F32)
        return (near + far).astype(BF16)

    grad_two = input_grad(delta_two)
    return input_grad(delta_one), grad_two


def solution(mesh):
    fine = Mesh(mesh.devices.reshape(4, 4, 4, 2, 2), ("zl", "y", "x", "zh", "c"))
    spec = P(("zl", "y", "x"), ("zh", "c"))
    return jax.shard_map(
        local,
        mesh=fine,
        in_specs=(spec, spec, P(None, ("zh", "c"))),
        out_specs=(spec, spec),
        check_vma=False,
    )
```

```python
import jax
import jax.numpy as jnp
from jax import lax
from jax.sharding import Mesh, PartitionSpec as P

OFF_WEIGHT = 0.0125
EPSILON = 1e-05
F32 = jnp.float32
BF16 = jnp.bfloat16
SWAP = [(0, 1), (1, 0)]
EXTRA = 16


def dot(left, right, left_dim, right_dim):
    return lax.dot_general(
        left, right, (((left_dim,), (right_dim,)), ((), ())), preferred_element_type=F32
    )


def swap(value, axis):
    return lax.ppermute(value, axis, SWAP)


def gather_zl(value):
    count = lax.axis_size("zl")
    return lax.all_to_all(
        jnp.broadcast_to(value[None], (count,) + value.shape), "zl", 0, 0, tiled=True
    )


def shift(value, axis, step):
    count = lax.axis_size(axis)
    return lax.ppermute(value, axis, [(i, (i + step) % count) for i in range(count)])


def small_gather_zl(value):
    return [value] + [shift(value, "zl", step) for step in range(1, lax.axis_size("zl"))]


def rotate(value, start):
    return lax.dynamic_slice_in_dim(jnp.concatenate([value, value], axis=1), start, value.shape[1], 1)


def scatter_columns(rotated, axis):
    count = lax.axis_size(axis)
    blocks = jnp.split(rotated, count, axis=1)
    return jnp.concatenate([blocks[0]] + [shift(blocks[k], axis, k) for k in range(1, count)], axis=0)


def gather_columns(stacked, axis):
    count = lax.axis_size(axis)
    blocks = jnp.split(stacked, count, axis=0)
    return jnp.concatenate([blocks[0]] + [shift(blocks[k], axis, -k) for k in range(1, count)], axis=1)


def spread(value, axis):
    return [value] + [shift(value, axis, k) for k in range(1, lax.axis_size(axis))]


def collect(pieces, axis):
    return sum(
        (piece if k == 0 else shift(piece, axis, -k)).astype(F32) for k, piece in enumerate(pieces)
    )


def combine(means, squares, rows):
    mean = sum(means) / len(means)
    return mean, sum(squares) + rows * sum((m - mean) ** 2 for m in means)


def moments(values):
    rows = values.shape[0]
    wide = values.astype(F32)
    mean = jnp.sum(wide, axis=0) / rows
    square = jnp.sum((wide - mean) ** 2, axis=0)
    parts = small_gather_zl(jnp.stack([mean, square]))
    return combine([p[0] for p in parts], [p[1] for p in parts], rows)


def split(vector, pieces):
    out = []
    for _ in range(pieces):
        high = lax.reduce_precision(vector, 8, 7)
        out.append(high.astype(BF16))
        vector = vector - high
    return out


def extra_rows(vectors):
    rows = [piece for vector, pieces in vectors for piece in split(vector, pieces)]
    stacked = jnp.stack(rows)
    return jnp.pad(stacked, ((0, EXTRA - len(rows)),) + ((0, 0),) * (stacked.ndim - 1))


def read_rows(rows, pieces):
    out, at = [], 0
    for count in pieces:
        out.append(sum(rows[at + k] for k in range(count)))
        at += count
    return out


def local(view_one, view_two, proj_weight):
    rows, width = view_one.shape
    n_zl, n_y, n_x = lax.axis_size("zl"), lax.axis_size("y"), lax.axis_size("x")
    n_plane = n_y * n_x
    total_rows = rows * n_zl * n_plane
    blk_i, blk_j = width // n_x, width // n_y
    core = lax.axis_index("c")
    zh = lax.axis_index("zh")

    at_x, at_y = lax.axis_index("x"), lax.axis_index("y")
    rotated_two = rotate(view_two, at_y * blk_j)
    crossed = swap(rotated_two, "zh")
    rotated_one = rotate(view_one, at_x * blk_i)
    plane_rows = n_plane * rows

    def plane_of_two(rotated):
        parts = spread(scatter_columns(rotated, "y"), "x")
        parts = [part.reshape(n_y, 1, rows, blk_j) for part in parts]
        return jnp.concatenate(parts, axis=1).reshape(plane_rows, blk_j)

    own_one = jnp.concatenate(spread(scatter_columns(rotated_one, "x"), "y"), axis=0)
    own = jnp.concatenate([own_one, plane_of_two(rotated_two)], axis=1)
    far_two = plane_of_two(crossed)

    def normalize(values, mean, rstd):
        return ((values.astype(F32) - mean) * rstd).astype(BF16)

    mean, square = moments(own)
    rstd = lax.rsqrt(square / total_rows + EPSILON)
    norm_own = normalize(own, mean, rstd)
    sums_own = jnp.sum(norm_own.astype(F32), axis=0)
    far_stats = swap(jnp.stack([mean[blk_i:], rstd[blk_i:], sums_own[blk_i:]]), "zh")
    sums_one = jnp.concatenate([sums_own[:blk_i], swap(sums_own[:blk_i], "c")])
    sums_two = jnp.concatenate([sums_own[blk_i:], far_stats[2]])
    norm_one = jnp.concatenate([norm_own[:, :blk_i], swap(norm_own[:, :blk_i], "c")], axis=1)
    norm_two = jnp.concatenate([norm_own[:, blk_i:], normalize(far_two, far_stats[0], far_stats[1])], axis=1)
    rstd_one, rstd_two = rstd[:blk_i], rstd[blk_i:]

    tile_i, tile_j = norm_one.shape[1], norm_two.shape[1]
    part = dot(norm_one, norm_two, 0, 0).astype(BF16).reshape(n_zl, tile_i // n_zl, tile_j)
    sums = extra_rows([(sums_one, 2), (sums_two, 2)])
    part = jnp.concatenate([part, jnp.broadcast_to(sums[None], (n_zl,) + sums.shape)], axis=1)
    part = jnp.sum(lax.all_to_all(part, "zl", 0, 0, tiled=True).astype(F32), axis=0)
    slice_i = tile_i // n_zl
    mu_one, mu_two = (v / total_rows for v in read_rows(part[slice_i:], (2, 2)))
    corr = part[:slice_i] / total_rows
    on_diag = lax.axis_index("x") == lax.axis_index("y")

    def diagonal(height, first):
        row_ids = first + lax.broadcasted_iota(jnp.int32, (height, tile_j), 0)
        col_ids = lax.broadcasted_iota(jnp.int32, (height, tile_j), 1)
        return (row_ids == col_ids) & (row_ids < blk_i) & on_diag

    grad = jnp.where(
        diagonal(slice_i, lax.axis_index("zl") * slice_i),
        -2.0 * (1.0 - corr),
        2.0 * OFF_WEIGHT * corr,
    ).astype(BF16)
    grad = gather_zl(grad).reshape(tile_i, tile_j)

    def products(grad):
        wide = grad.astype(F32)
        return wide, wide * jnp.where(diagonal(tile_i, 0), 1.0 + 0.5 * wide, wide / (2.0 * OFF_WEIGHT))

    def delta(normal, upstream, cross, mean_up, rstd):
        return (rstd * (upstream - mean_up - normal.astype(F32) * cross)).astype(BF16)

    def with_extra(piece, extra):
        return jnp.concatenate([piece.reshape(-1, piece.shape[-1]), extra], axis=0)

    wide, product = products(grad)
    cross_one, mean_up_one = jnp.sum(product, axis=1), jnp.sum(wide * mu_two[None, :], axis=1)
    up_one = dot(norm_two, grad, 1, 1)
    other = with_extra(
        up_one[:, blk_i:].astype(BF16), extra_rows([(cross_one[blk_i:], 2), (mean_up_one[blk_i:], 2)])
    )
    other, grad = lax.optimization_barrier((other, grad))
    other = swap(other, "c")

    wide, product = products(grad)
    cross_two, mean_up_two = jnp.sum(product, axis=0), jnp.sum(wide * mu_one[:, None], axis=0)
    up_two = dot(norm_one, grad, 1, 0).astype(BF16).reshape(n_y, n_x, rows, tile_j)

    def for_x(columns):
        extra = extra_rows([(cross_two[columns], 2), (mean_up_two[columns], 2)])
        return [with_extra(up_two[:, k, :, columns], extra) for k in range(n_x)]

    pieces_far, pieces_near = for_x(slice(blk_j, None)), for_x(slice(0, blk_j))
    other, pieces_far, pieces_near = lax.optimization_barrier((other, pieces_far, pieces_near))

    other = other.astype(F32)
    up_one = (up_one[:, :blk_i] + other[:plane_rows]).astype(BF16).reshape(n_y, n_x * rows, blk_i)
    tail = read_rows(other[plane_rows:], (2, 2))
    extra = extra_rows([(cross_one[:blk_i] + tail[0], 2), (mean_up_one[:blk_i] + tail[1], 2)])
    pieces_one = [with_extra(up_one[k], extra) for k in range(n_y)]
    pieces_one, pieces_far = lax.optimization_barrier((pieces_one, pieces_far))

    part_rows = n_y * rows
    far = collect(pieces_far, "x")
    far = with_extra(
        far[:part_rows].astype(BF16), extra_rows([(v, 2) for v in read_rows(far[part_rows:], (2, 2))])
    )
    far, pieces_near = lax.optimization_barrier((far, pieces_near))
    far = swap(far, "zh").astype(F32)

    up_one = collect(pieces_one, "y")
    cross_one, mean_up_one = read_rows(up_one[n_x * rows :], (2, 2))
    delta_one = delta(
        norm_one[: n_x * rows, :blk_i], up_one[: n_x * rows], cross_one, mean_up_one, rstd_one
    )
    delta_one = rotate(gather_columns(delta_one, "x"), ((n_x - at_x) % n_x) * blk_i)

    near = collect(pieces_near, "x")
    up_two = near[:part_rows] + far[:part_rows]
    cross_two, mean_up_two = (
        a + b for a, b in zip(read_rows(near[part_rows:], (2, 2)), read_rows(far[part_rows:], (2, 2)))
    )
    normal = norm_two.reshape(n_y, n_x, rows, tile_j)[:, 0, :, :blk_j].reshape(part_rows, blk_j)
    delta_two = delta(normal, up_two, cross_two, mean_up_two, rstd_two)
    delta_two = rotate(gather_columns(delta_two, "y"), ((n_y - at_y) % n_y) * blk_j)

    weight = proj_weight.reshape(2, 2, width, width)

    def block(half, member):
        return lax.dynamic_slice(weight, (half, member, 0, 0), (1, 1, width, width)).reshape(width, width)

    far_give, far_keep = block(1 - zh, 1 - core), block(1 - zh, core)
    near_give, near_keep = block(zh, 1 - core), block(zh, core)

    def input_grad(value):
        far = dot(value, far_keep, 1, 1) + swap(dot(value, far_give, 1, 1).astype(BF16), "c").astype(F32)
        far = swap(far.astype(BF16), "zh").astype(F32)
        near = dot(value, near_keep, 1, 1) + swap(dot(value, near_give, 1, 1).astype(BF16), "c").astype(F32)
        return (near + far).astype(BF16)

    grad_two = input_grad(delta_two)
    return input_grad(delta_one), grad_two


def solution(mesh):
    fine = Mesh(mesh.devices.reshape(4, 4, 4, 2, 2), ("zl", "y", "x", "zh", "c"))
    spec = P(("zl", "y", "x"), ("zh", "c"))
    return jax.shard_map(
        local,
        mesh=fine,
        in_specs=(spec, spec, P(None, ("zh", "c"))),
        out_specs=(spec, spec),
        check_vma=False,
    )
```

```python
import jax
import jax.numpy as jnp
from jax import lax
from jax.sharding import Mesh, PartitionSpec as P

OFF_WEIGHT = 0.0125
EPSILON = 1e-05
F32 = jnp.float32
BF16 = jnp.bfloat16
SWAP = [(0, 1), (1, 0)]
EXTRA = 16


def dot(left, right, left_dim, right_dim):
    return lax.dot_general(
        left, right, (((left_dim,), (right_dim,)), ((), ())), preferred_element_type=F32
    )


def swap(value, axis):
    return lax.ppermute(value, axis, SWAP)


def gather_zl(value):
    count = lax.axis_size("zl")
    return lax.all_to_all(
        jnp.broadcast_to(value[None], (count,) + value.shape), "zl", 0, 0, tiled=True
    )


def shift(value, axis, step):
    count = lax.axis_size(axis)
    return lax.ppermute(value, axis, [(i, (i + step) % count) for i in range(count)])


def small_gather_zl(value):
    return [value] + [shift(value, "zl", step) for step in range(1, lax.axis_size("zl"))]


def rotate(value, start):
    return lax.dynamic_slice_in_dim(jnp.concatenate([value, value], axis=1), start, value.shape[1], 1)


def scatter_columns(rotated, axis):
    count = lax.axis_size(axis)
    blocks = jnp.split(rotated, count, axis=1)
    return jnp.concatenate([blocks[0]] + [shift(blocks[k], axis, k) for k in range(1, count)], axis=0)


def gather_columns(stacked, axis):
    count = lax.axis_size(axis)
    blocks = jnp.split(stacked, count, axis=0)
    return jnp.concatenate([blocks[0]] + [shift(blocks[k], axis, -k) for k in range(1, count)], axis=1)


def trade_columns(view, axis):
    count = lax.axis_size(axis)
    slots = jnp.stack(jnp.split(view, count, axis=1))
    out = lax.all_to_all(slots, axis, 0, 0, tiled=True)[::-1]
    out = lax.dynamic_slice_in_dim(
        jnp.concatenate([out, out]), count - 1 - lax.axis_index(axis), count, 0
    )
    return out.reshape(-1, out.shape[2])


def spread(value, axis):
    return [value] + [shift(value, axis, k) for k in range(1, lax.axis_size(axis))]


def collect(pieces, axis):
    return sum(
        (piece if k == 0 else shift(piece, axis, -k)).astype(F32) for k, piece in enumerate(pieces)
    )


def combine(means, squares, rows):
    mean = sum(means) / len(means)
    return mean, sum(squares) + rows * sum((m - mean) ** 2 for m in means)


def moments(values):
    rows = values.shape[0]
    wide = values.astype(F32)
    mean = jnp.sum(wide, axis=0) / rows
    square = jnp.sum((wide - mean) ** 2, axis=0)
    parts = small_gather_zl(jnp.stack([mean, square]))
    return combine([p[0] for p in parts], [p[1] for p in parts], rows)


def split(vector, pieces):
    out = []
    for _ in range(pieces):
        high = lax.reduce_precision(vector, 8, 7)
        out.append(high.astype(BF16))
        vector = vector - high
    return out


def extra_rows(vectors):
    rows = [piece for vector, pieces in vectors for piece in split(vector, pieces)]
    stacked = jnp.stack(rows)
    return jnp.pad(stacked, ((0, EXTRA - len(rows)),) + ((0, 0),) * (stacked.ndim - 1))


def read_rows(rows, pieces):
    out, at = [], 0
    for count in pieces:
        out.append(sum(rows[at + k] for k in range(count)))
        at += count
    return out


def local(view_one, view_two, proj_weight):
    rows, width = view_one.shape
    n_zl, n_y, n_x = lax.axis_size("zl"), lax.axis_size("y"), lax.axis_size("x")
    n_plane = n_y * n_x
    total_rows = rows * n_zl * n_plane
    blk_i, blk_j = width // n_x, width // n_y
    core = lax.axis_index("c")
    zh = lax.axis_index("zh")

    at_x, at_y = lax.axis_index("x"), lax.axis_index("y")
    crossed = swap(view_two, "zh")
    rotated_two = rotate(view_two, at_y * blk_j)
    plane_rows = n_plane * rows

    def plane_of_two(part):
        parts = [part.reshape(n_y, 1, rows, blk_j) for part in spread(part, "x")]
        return jnp.concatenate(parts, axis=1).reshape(plane_rows, blk_j)

    own_one = jnp.concatenate(spread(trade_columns(view_one, "x"), "y"), axis=0)
    own = jnp.concatenate([own_one, plane_of_two(scatter_columns(rotated_two, "y"))], axis=1)
    far_two = plane_of_two(trade_columns(crossed, "y"))

    def normalize(values, mean, rstd):
        return ((values.astype(F32) - mean) * rstd).astype(BF16)

    mean, square = moments(own)
    rstd = lax.rsqrt(square / total_rows + EPSILON)
    norm_own = normalize(own, mean, rstd)
    sums_own = jnp.sum(norm_own.astype(F32), axis=0)
    far_stats = swap(jnp.stack([mean[blk_i:], rstd[blk_i:], sums_own[blk_i:]]), "zh")
    sums_one = jnp.concatenate([sums_own[:blk_i], swap(sums_own[:blk_i], "c")])
    sums_two = jnp.concatenate([sums_own[blk_i:], far_stats[2]])
    norm_one = jnp.concatenate([norm_own[:, :blk_i], swap(norm_own[:, :blk_i], "c")], axis=1)
    norm_two = jnp.concatenate([norm_own[:, blk_i:], normalize(far_two, far_stats[0], far_stats[1])], axis=1)
    rstd_one, rstd_two = rstd[:blk_i], rstd[blk_i:]

    tile_i, tile_j = norm_one.shape[1], norm_two.shape[1]
    part = dot(norm_one, norm_two, 0, 0).astype(BF16).reshape(n_zl, tile_i // n_zl, tile_j)
    sums = extra_rows([(sums_one, 2), (sums_two, 2)])
    part = jnp.concatenate([part, jnp.broadcast_to(sums[None], (n_zl,) + sums.shape)], axis=1)
    part = jnp.sum(lax.all_to_all(part, "zl", 0, 0, tiled=True).astype(F32), axis=0)
    slice_i = tile_i // n_zl
    mu_one, mu_two = (v / total_rows for v in read_rows(part[slice_i:], (2, 2)))
    corr = part[:slice_i] / total_rows
    on_diag = lax.axis_index("x") == lax.axis_index("y")

    def diagonal(height, first):
        row_ids = first + lax.broadcasted_iota(jnp.int32, (height, tile_j), 0)
        col_ids = lax.broadcasted_iota(jnp.int32, (height, tile_j), 1)
        return (row_ids == col_ids) & (row_ids < blk_i) & on_diag

    grad = jnp.where(
        diagonal(slice_i, lax.axis_index("zl") * slice_i),
        -2.0 * (1.0 - corr),
        2.0 * OFF_WEIGHT * corr,
    ).astype(BF16)
    grad = gather_zl(grad).reshape(tile_i, tile_j)

    def products(grad):
        wide = grad.astype(F32)
        return wide, wide * jnp.where(diagonal(tile_i, 0), 1.0 + 0.5 * wide, wide / (2.0 * OFF_WEIGHT))

    def delta(normal, upstream, cross, mean_up, rstd):
        return (rstd * (upstream - mean_up - normal.astype(F32) * cross)).astype(BF16)

    def with_extra(piece, extra):
        return jnp.concatenate([piece.reshape(-1, piece.shape[-1]), extra], axis=0)

    wide, product = products(grad)
    cross_one, mean_up_one = jnp.sum(product, axis=1), jnp.sum(wide * mu_two[None, :], axis=1)
    up_one = dot(norm_two, grad, 1, 1)
    other = with_extra(
        up_one[:, blk_i:].astype(BF16), extra_rows([(cross_one[blk_i:], 2), (mean_up_one[blk_i:], 2)])
    )
    other, grad = lax.optimization_barrier((other, grad))
    other = swap(other, "c")

    wide, product = products(grad)
    cross_two, mean_up_two = jnp.sum(product, axis=0), jnp.sum(wide * mu_one[:, None], axis=0)
    up_two = dot(norm_one, grad, 1, 0).astype(BF16).reshape(n_y, n_x, rows, tile_j)

    def for_x(columns):
        extra = extra_rows([(cross_two[columns], 2), (mean_up_two[columns], 2)])
        return [with_extra(up_two[:, k, :, columns], extra) for k in range(n_x)]

    pieces_far, pieces_near = for_x(slice(blk_j, None)), for_x(slice(0, blk_j))
    other, pieces_far, pieces_near = lax.optimization_barrier((other, pieces_far, pieces_near))

    other = other.astype(F32)
    up_one = (up_one[:, :blk_i] + other[:plane_rows]).astype(BF16).reshape(n_y, n_x * rows, blk_i)
    tail = read_rows(other[plane_rows:], (2, 2))
    extra = extra_rows([(cross_one[:blk_i] + tail[0], 2), (mean_up_one[:blk_i] + tail[1], 2)])
    pieces_one = [with_extra(up_one[k], extra) for k in range(n_y)]
    pieces_one, pieces_far = lax.optimization_barrier((pieces_one, pieces_far))

    weight = proj_weight.reshape(2, 2, width, width)

    def block(half, member):
        return lax.dynamic_slice(weight, (half, member, 0, 0), (1, 1, width, width)).reshape(width, width)

    far_give, far_keep = block(1 - zh, 1 - core), block(1 - zh, core)
    near_give, near_keep = block(zh, 1 - core), block(zh, core)

    def sum_cores(value, keep, give):
        return dot(value, keep, 1, 1) + swap(dot(value, give, 1, 1).astype(BF16), "c").astype(F32)

    part_rows = n_y * rows
    far = collect(pieces_far, "x")
    far = with_extra(
        far[:part_rows].astype(BF16), extra_rows([(v, 2) for v in read_rows(far[part_rows:], (2, 2))])
    )
    far, pieces_near = lax.optimization_barrier((far, pieces_near))
    far = swap(far, "zh")

    up_one = collect(pieces_one, "y")
    cross_one, mean_up_one = read_rows(up_one[n_x * rows :], (2, 2))
    delta_one = delta(
        norm_one[: n_x * rows, :blk_i], up_one[: n_x * rows], cross_one, mean_up_one, rstd_one
    )
    delta_one = rotate(gather_columns(delta_one, "x"), ((n_x - at_x) % n_x) * blk_i)
    far_one = sum_cores(delta_one, far_keep, far_give).astype(BF16)
    far, far_one = lax.optimization_barrier((far, far_one))
    far_one = swap(far_one, "zh")
    near_one = sum_cores(delta_one, near_keep, near_give)
    far = far.astype(F32)

    near = collect(pieces_near, "x")
    up_two = near[:part_rows] + far[:part_rows]
    cross_two, mean_up_two = (
        a + b for a, b in zip(read_rows(near[part_rows:], (2, 2)), read_rows(far[part_rows:], (2, 2)))
    )
    normal = norm_two.reshape(n_y, n_x, rows, tile_j)[:, 0, :, :blk_j].reshape(part_rows, blk_j)
    delta_two = delta(normal, up_two, cross_two, mean_up_two, rstd_two)
    delta_two = rotate(gather_columns(delta_two, "y"), ((n_y - at_y) % n_y) * blk_j)
    far_two = swap(sum_cores(delta_two, far_keep, far_give).astype(BF16), "zh")
    near_two = sum_cores(delta_two, near_keep, near_give)
    return (
        (near_one + far_one.astype(F32)).astype(BF16),
        (near_two + far_two.astype(F32)).astype(BF16),
    )


def solution(mesh):
    fine = Mesh(mesh.devices.reshape(4, 4, 4, 2, 2), ("zl", "y", "x", "zh", "c"))
    spec = P(("zl", "y", "x"), ("zh", "c"))
    return jax.shard_map(
        local,
        mesh=fine,
        in_specs=(spec, spec, P(None, ("zh", "c"))),
        out_specs=(spec, spec),
        check_vma=False,
    )
```

```python
import jax
import jax.numpy as jnp
from jax import lax
from jax.sharding import Mesh, PartitionSpec as P

OFF_WEIGHT = 0.0125
EPSILON = 1e-05
F32 = jnp.float32
BF16 = jnp.bfloat16
SWAP = [(0, 1), (1, 0)]
EXTRA = 16


def dot(left, right, left_dim, right_dim):
    return lax.dot_general(
        left, right, (((left_dim,), (right_dim,)), ((), ())), preferred_element_type=F32
    )


def swap(value, axis):
    return lax.ppermute(value, axis, SWAP)


def gather_zl(value):
    count = lax.axis_size("zl")
    return lax.all_to_all(
        jnp.broadcast_to(value[None], (count,) + value.shape), "zl", 0, 0, tiled=True
    )


def shift(value, axis, step):
    count = lax.axis_size(axis)
    return lax.ppermute(value, axis, [(i, (i + step) % count) for i in range(count)])


def small_gather_zl(value):
    return [value] + [shift(value, "zl", step) for step in range(1, lax.axis_size("zl"))]


def rotate(value, start):
    return lax.dynamic_slice_in_dim(jnp.concatenate([value, value], axis=1), start, value.shape[1], 1)


def scatter_columns(rotated, axis):
    count = lax.axis_size(axis)
    blocks = jnp.split(rotated, count, axis=1)
    return jnp.concatenate([blocks[0]] + [shift(blocks[k], axis, k) for k in range(1, count)], axis=0)


def gather_columns(stacked, axis):
    count = lax.axis_size(axis)
    blocks = jnp.split(stacked, count, axis=0)
    return jnp.concatenate([blocks[0]] + [shift(blocks[k], axis, -k) for k in range(1, count)], axis=1)


def trade_back(chunks, axis):
    count = lax.axis_size(axis)
    chunks = chunks[::-1]
    slots = lax.dynamic_slice_in_dim(
        jnp.concatenate([chunks, chunks]), count - 1 - lax.axis_index(axis), count, 0
    )
    out = lax.all_to_all(slots, axis, 0, 0, tiled=True)
    return jnp.concatenate([out[k] for k in range(count)], axis=1)


def spread(value, axis):
    return [value] + [shift(value, axis, k) for k in range(1, lax.axis_size(axis))]


def collect(pieces, axis):
    return sum(
        (piece if k == 0 else shift(piece, axis, -k)).astype(F32) for k, piece in enumerate(pieces)
    )


def combine(means, squares, rows):
    mean = sum(means) / len(means)
    return mean, sum(squares) + rows * sum((m - mean) ** 2 for m in means)


def moments(values):
    rows = values.shape[0]
    wide = values.astype(F32)
    mean = jnp.sum(wide, axis=0) / rows
    square = jnp.sum((wide - mean) ** 2, axis=0)
    parts = small_gather_zl(jnp.stack([mean, square]))
    return combine([p[0] for p in parts], [p[1] for p in parts], rows)


def split(vector, pieces):
    out = []
    for _ in range(pieces):
        high = lax.reduce_precision(vector, 8, 7)
        out.append(high.astype(BF16))
        vector = vector - high
    return out


def extra_rows(vectors):
    rows = [piece for vector, pieces in vectors for piece in split(vector, pieces)]
    stacked = jnp.stack(rows)
    return jnp.pad(stacked, ((0, EXTRA - len(rows)),) + ((0, 0),) * (stacked.ndim - 1))


def read_rows(rows, pieces):
    out, at = [], 0
    for count in pieces:
        out.append(sum(rows[at + k] for k in range(count)))
        at += count
    return out


def local(view_one, view_two, proj_weight):
    rows, width = view_one.shape
    n_zl, n_y, n_x = lax.axis_size("zl"), lax.axis_size("y"), lax.axis_size("x")
    n_plane = n_y * n_x
    total_rows = rows * n_zl * n_plane
    blk_i, blk_j = width // n_x, width // n_y
    core = lax.axis_index("c")
    zh = lax.axis_index("zh")

    at_x, at_y = lax.axis_index("x"), lax.axis_index("y")
    rotated_two = rotate(view_two, at_y * blk_j)
    crossed = swap(rotated_two, "zh")
    rotated_one = rotate(view_one, at_x * blk_i)
    plane_rows = n_plane * rows

    def plane_of_two(rotated):
        parts = spread(scatter_columns(rotated, "y"), "x")
        parts = [part.reshape(n_y, 1, rows, blk_j) for part in parts]
        return jnp.concatenate(parts, axis=1).reshape(plane_rows, blk_j)

    own_one = jnp.concatenate(spread(scatter_columns(rotated_one, "x"), "y"), axis=0)
    own = jnp.concatenate([own_one, plane_of_two(rotated_two)], axis=1)
    far_two = plane_of_two(crossed)

    def normalize(values, mean, rstd):
        return ((values.astype(F32) - mean) * rstd).astype(BF16)

    mean, square = moments(own)
    rstd = lax.rsqrt(square / total_rows + EPSILON)
    norm_own = normalize(own, mean, rstd)
    sums_own = jnp.sum(norm_own.astype(F32), axis=0)
    far_stats = swap(jnp.stack([mean[blk_i:], rstd[blk_i:], sums_own[blk_i:]]), "zh")
    sums_one = jnp.concatenate([sums_own[:blk_i], swap(sums_own[:blk_i], "c")])
    sums_two = jnp.concatenate([sums_own[blk_i:], far_stats[2]])
    norm_one = jnp.concatenate([norm_own[:, :blk_i], swap(norm_own[:, :blk_i], "c")], axis=1)
    norm_two = jnp.concatenate([norm_own[:, blk_i:], normalize(far_two, far_stats[0], far_stats[1])], axis=1)
    rstd_one, rstd_two = rstd[:blk_i], rstd[blk_i:]

    tile_i, tile_j = norm_one.shape[1], norm_two.shape[1]
    part = dot(norm_one, norm_two, 0, 0).astype(BF16).reshape(n_zl, tile_i // n_zl, tile_j)
    sums = extra_rows([(sums_one, 2), (sums_two, 2)])
    part = jnp.concatenate([part, jnp.broadcast_to(sums[None], (n_zl,) + sums.shape)], axis=1)
    part = jnp.sum(lax.all_to_all(part, "zl", 0, 0, tiled=True).astype(F32), axis=0)
    slice_i = tile_i // n_zl
    mu_one, mu_two = (v / total_rows for v in read_rows(part[slice_i:], (2, 2)))
    corr = part[:slice_i] / total_rows
    on_diag = lax.axis_index("x") == lax.axis_index("y")

    def diagonal(height, first):
        row_ids = first + lax.broadcasted_iota(jnp.int32, (height, tile_j), 0)
        col_ids = lax.broadcasted_iota(jnp.int32, (height, tile_j), 1)
        return (row_ids == col_ids) & (row_ids < blk_i) & on_diag

    grad = jnp.where(
        diagonal(slice_i, lax.axis_index("zl") * slice_i),
        -2.0 * (1.0 - corr),
        2.0 * OFF_WEIGHT * corr,
    ).astype(BF16)
    grad = gather_zl(grad).reshape(tile_i, tile_j)

    def products(grad):
        wide = grad.astype(F32)
        return wide, wide * jnp.where(diagonal(tile_i, 0), 1.0 + 0.5 * wide, wide / (2.0 * OFF_WEIGHT))

    def delta(normal, upstream, cross, mean_up, rstd):
        return (rstd * (upstream - mean_up - normal.astype(F32) * cross)).astype(BF16)

    def with_extra(piece, extra):
        return jnp.concatenate([piece.reshape(-1, piece.shape[-1]), extra], axis=0)

    part_rows = n_y * rows

    def for_x(grad, columns):
        wide, product = products(grad)
        cross, mean_up = jnp.sum(product, axis=0), jnp.sum(wide * mu_one[:, None], axis=0)
        extra = extra_rows([(cross[columns], 2), (mean_up[columns], 2)])
        upstream = dot(norm_one, grad[:, columns], 1, 0).astype(BF16).reshape(n_y, n_x, rows, -1)
        return [with_extra(upstream[:, k], extra) for k in range(n_x)]

    pieces_far, grad = lax.optimization_barrier((for_x(grad, slice(blk_j, None)), grad))
    far = collect(pieces_far, "x")
    far = with_extra(
        far[:part_rows].astype(BF16), extra_rows([(v, 2) for v in read_rows(far[part_rows:], (2, 2))])
    )

    wide, product = products(grad)
    cross_one, mean_up_one = jnp.sum(product, axis=1), jnp.sum(wide * mu_two[None, :], axis=1)
    other = with_extra(
        dot(norm_two, grad[blk_i:], 1, 1).astype(BF16),
        extra_rows([(cross_one[blk_i:], 2), (mean_up_one[blk_i:], 2)]),
    )
    other, grad = lax.optimization_barrier((other, grad))
    other = swap(other, "c").astype(F32)
    up_one = (dot(norm_two, grad[:blk_i], 1, 1) + other[:plane_rows]).astype(BF16)
    up_one = up_one.reshape(n_y, n_x * rows, blk_i)
    tail = read_rows(other[plane_rows:], (2, 2))
    extra = extra_rows([(cross_one[:blk_i] + tail[0], 2), (mean_up_one[:blk_i] + tail[1], 2)])
    pieces_one, grad = lax.optimization_barrier(([with_extra(up_one[k], extra) for k in range(n_y)], grad))
    pieces_near = for_x(grad, slice(0, blk_j))
    far, pieces_near = lax.optimization_barrier((far, pieces_near))
    far = swap(far, "zh").astype(F32)
    near = collect(pieces_near, "x")

    up_one = collect(pieces_one, "y")
    cross_one, mean_up_one = read_rows(up_one[n_x * rows :], (2, 2))
    delta_one = delta(
        norm_one[: n_x * rows, :blk_i], up_one[: n_x * rows], cross_one, mean_up_one, rstd_one
    )
    delta_one = trade_back(delta_one.reshape(n_x, rows, blk_i), "x")
    near, delta_one = lax.optimization_barrier((near, delta_one))

    up_two = near[:part_rows] + far[:part_rows]
    cross_two, mean_up_two = (
        a + b for a, b in zip(read_rows(near[part_rows:], (2, 2)), read_rows(far[part_rows:], (2, 2)))
    )
    normal = norm_two.reshape(n_y, n_x, rows, tile_j)[:, 0, :, :blk_j].reshape(part_rows, blk_j)
    delta_two = delta(normal, up_two, cross_two, mean_up_two, rstd_two)
    delta_two = rotate(gather_columns(delta_two, "y"), ((n_y - at_y) % n_y) * blk_j)

    weight = proj_weight.reshape(2, 2, width, width)

    def block(half, member):
        return lax.dynamic_slice(weight, (half, member, 0, 0), (1, 1, width, width)).reshape(width, width)

    far_give, far_keep = block(1 - zh, 1 - core), block(1 - zh, core)
    near_give, near_keep = block(zh, 1 - core), block(zh, core)

    def input_grad(value):
        far = dot(value, far_keep, 1, 1) + swap(dot(value, far_give, 1, 1).astype(BF16), "c").astype(F32)
        far = swap(far.astype(BF16), "zh").astype(F32)
        near = dot(value, near_keep, 1, 1) + swap(dot(value, near_give, 1, 1).astype(BF16), "c").astype(F32)
        return (near + far).astype(BF16)

    grad_two = input_grad(delta_two)
    return input_grad(delta_one), grad_two


def solution(mesh):
    fine = Mesh(mesh.devices.reshape(4, 4, 4, 2, 2), ("zl", "y", "x", "zh", "c"))
    spec = P(("zl", "y", "x"), ("zh", "c"))
    return jax.shard_map(
        local,
        mesh=fine,
        in_specs=(spec, spec, P(None, ("zh", "c"))),
        out_specs=(spec, spec),
        check_vma=False,
    )
```

```python
import jax
import jax.numpy as jnp
from jax import lax
from jax.sharding import Mesh, PartitionSpec as P

OFF_WEIGHT = 0.0125
EPSILON = 1e-05
F32 = jnp.float32
BF16 = jnp.bfloat16
SWAP = [(0, 1), (1, 0)]
EXTRA = 16


def dot(left, right, left_dim, right_dim):
    return lax.dot_general(
        left, right, (((left_dim,), (right_dim,)), ((), ())), preferred_element_type=F32
    )


def swap(value, axis):
    return lax.ppermute(value, axis, SWAP)


def gather_zl(value):
    count = lax.axis_size("zl")
    return lax.all_to_all(
        jnp.broadcast_to(value[None], (count,) + value.shape), "zl", 0, 0, tiled=True
    )


def shift(value, axis, step):
    count = lax.axis_size(axis)
    return lax.ppermute(value, axis, [(i, (i + step) % count) for i in range(count)])


def small_gather_zl(value):
    return [value] + [shift(value, "zl", step) for step in range(1, lax.axis_size("zl"))]


def rotate(value, start):
    return lax.dynamic_slice_in_dim(jnp.concatenate([value, value], axis=1), start, value.shape[1], 1)


def scatter_columns(rotated, axis):
    count = lax.axis_size(axis)
    blocks = jnp.split(rotated, count, axis=1)
    return jnp.concatenate([blocks[0]] + [shift(blocks[k], axis, k) for k in range(1, count)], axis=0)


def gather_columns(stacked, axis):
    count = lax.axis_size(axis)
    blocks = jnp.split(stacked, count, axis=0)
    return jnp.concatenate([blocks[0]] + [shift(blocks[k], axis, -k) for k in range(1, count)], axis=1)


def trade_back(chunks, axis):
    count = lax.axis_size(axis)
    chunks = chunks[::-1]
    slots = lax.dynamic_slice_in_dim(
        jnp.concatenate([chunks, chunks]), count - 1 - lax.axis_index(axis), count, 0
    )
    out = lax.all_to_all(slots, axis, 0, 0, tiled=True)
    return jnp.concatenate([out[k] for k in range(count)], axis=1)


def spread(value, axis):
    return [value] + [shift(value, axis, k) for k in range(1, lax.axis_size(axis))]


def collect(pieces, axis):
    return sum(
        (piece if k == 0 else shift(piece, axis, -k)).astype(F32) for k, piece in enumerate(pieces)
    )


def combine(means, squares, rows):
    mean = sum(means) / len(means)
    return mean, sum(squares) + rows * sum((m - mean) ** 2 for m in means)


def moments(values):
    rows = values.shape[0]
    wide = values.astype(F32)
    mean = jnp.sum(wide, axis=0) / rows
    square = jnp.sum((wide - mean) ** 2, axis=0)
    parts = small_gather_zl(jnp.stack([mean, square]))
    return combine([p[0] for p in parts], [p[1] for p in parts], rows)


def split(vector, pieces):
    out = []
    for _ in range(pieces):
        high = lax.reduce_precision(vector, 8, 7)
        out.append(high.astype(BF16))
        vector = vector - high
    return out


def extra_rows(vectors):
    rows = [piece for vector, pieces in vectors for piece in split(vector, pieces)]
    stacked = jnp.stack(rows)
    return jnp.pad(stacked, ((0, EXTRA - len(rows)),) + ((0, 0),) * (stacked.ndim - 1))


def read_rows(rows, pieces):
    out, at = [], 0
    for count in pieces:
        out.append(sum(rows[at + k] for k in range(count)))
        at += count
    return out


def local(view_one, view_two, proj_weight):
    rows, width = view_one.shape
    n_zl, n_y, n_x = lax.axis_size("zl"), lax.axis_size("y"), lax.axis_size("x")
    n_plane = n_y * n_x
    total_rows = rows * n_zl * n_plane
    blk_i, blk_j = width // n_x, width // n_y
    core = lax.axis_index("c")
    zh = lax.axis_index("zh")

    at_x, at_y = lax.axis_index("x"), lax.axis_index("y")
    rotated_two = rotate(view_two, at_y * blk_j)
    crossed = swap(rotated_two, "zh")
    rotated_one = rotate(view_one, at_x * blk_i)
    plane_rows = n_plane * rows

    def plane_of_two(rotated):
        parts = spread(scatter_columns(rotated, "y"), "x")
        parts = [part.reshape(n_y, 1, rows, blk_j) for part in parts]
        return jnp.concatenate(parts, axis=1).reshape(plane_rows, blk_j)

    own_one = jnp.concatenate(spread(scatter_columns(rotated_one, "x"), "y"), axis=0)
    own = jnp.concatenate([own_one, plane_of_two(rotated_two)], axis=1)
    far_two = plane_of_two(crossed)

    def normalize(values, mean, rstd):
        return ((values.astype(F32) - mean) * rstd).astype(BF16)

    mean, square = moments(own)
    rstd = lax.rsqrt(square / total_rows + EPSILON)
    norm_own = normalize(own, mean, rstd)
    sums_own = jnp.sum(norm_own.astype(F32), axis=0)
    far_stats = swap(jnp.stack([mean[blk_i:], rstd[blk_i:], sums_own[blk_i:]]), "zh")
    sums_one = jnp.concatenate([sums_own[:blk_i], swap(sums_own[:blk_i], "c")])
    sums_two = jnp.concatenate([sums_own[blk_i:], far_stats[2]])
    norm_one = jnp.concatenate([norm_own[:, :blk_i], swap(norm_own[:, :blk_i], "c")], axis=1)
    norm_two = jnp.concatenate([norm_own[:, blk_i:], normalize(far_two, far_stats[0], far_stats[1])], axis=1)
    rstd_one, rstd_two = rstd[:blk_i], rstd[blk_i:]

    tile_i, tile_j = norm_one.shape[1], norm_two.shape[1]
    part = dot(norm_one, norm_two, 0, 0).astype(BF16).reshape(n_zl, tile_i // n_zl, tile_j)
    sums = extra_rows([(sums_one, 2), (sums_two, 2)])
    part = jnp.concatenate([part, jnp.broadcast_to(sums[None], (n_zl,) + sums.shape)], axis=1)
    part = jnp.sum(lax.all_to_all(part, "zl", 0, 0, tiled=True).astype(F32), axis=0)
    slice_i = tile_i // n_zl
    mu_one, mu_two = (v / total_rows for v in read_rows(part[slice_i:], (2, 2)))
    corr = part[:slice_i] / total_rows
    on_diag = lax.axis_index("x") == lax.axis_index("y")

    def diagonal(height, first):
        row_ids = first + lax.broadcasted_iota(jnp.int32, (height, tile_j), 0)
        col_ids = lax.broadcasted_iota(jnp.int32, (height, tile_j), 1)
        return (row_ids == col_ids) & (row_ids < blk_i) & on_diag

    grad = jnp.where(
        diagonal(slice_i, lax.axis_index("zl") * slice_i),
        -2.0 * (1.0 - corr),
        2.0 * OFF_WEIGHT * corr,
    ).astype(BF16)
    grad = gather_zl(grad).reshape(tile_i, tile_j)

    weight = proj_weight.reshape(2, 2, width, width)

    def block(half, member):
        return lax.dynamic_slice(weight, (half, member, 0, 0), (1, 1, width, width)).reshape(width, width)

    far_give, far_keep = block(1 - zh, 1 - core), block(1 - zh, core)
    near_give, near_keep = block(zh, 1 - core), block(zh, core)
    blocks = (far_give, far_keep, near_give, near_keep)
    (far_give, far_keep, near_give, near_keep), grad = lax.optimization_barrier((blocks, grad))

    def products(grad):
        wide = grad.astype(F32)
        return wide, wide * jnp.where(diagonal(tile_i, 0), 1.0 + 0.5 * wide, wide / (2.0 * OFF_WEIGHT))

    def delta(normal, upstream, cross, mean_up, rstd):
        return (rstd * (upstream - mean_up - normal.astype(F32) * cross)).astype(BF16)

    def with_extra(piece, extra):
        return jnp.concatenate([piece.reshape(-1, piece.shape[-1]), extra], axis=0)

    part_rows = n_y * rows

    def for_x(grad, columns):
        wide, product = products(grad)
        cross, mean_up = jnp.sum(product, axis=0), jnp.sum(wide * mu_one[:, None], axis=0)
        extra = extra_rows([(cross[columns], 2), (mean_up[columns], 2)])
        upstream = dot(norm_one, grad[:, columns], 1, 0).astype(BF16).reshape(n_y, n_x, rows, -1)
        return [with_extra(upstream[:, k], extra) for k in range(n_x)]

    pieces_far, grad = lax.optimization_barrier((for_x(grad, slice(blk_j, None)), grad))
    parts_far = [piece if k == 0 else shift(piece, "x", -k) for k, piece in enumerate(pieces_far)]

    wide, product = products(grad)
    cross_one, mean_up_one = jnp.sum(product, axis=1), jnp.sum(wide * mu_two[None, :], axis=1)
    other = with_extra(
        dot(norm_two, grad[blk_i:], 1, 1).astype(BF16),
        extra_rows([(cross_one[blk_i:], 2), (mean_up_one[blk_i:], 2)]),
    )
    other, grad = lax.optimization_barrier((other, grad))
    other = swap(other, "c").astype(F32)
    up_one = (dot(norm_two, grad[:blk_i], 1, 1) + other[:plane_rows]).astype(BF16)
    up_one = up_one.reshape(n_y, n_x * rows, blk_i)
    tail = read_rows(other[plane_rows:], (2, 2))
    extra = extra_rows([(cross_one[:blk_i] + tail[0], 2), (mean_up_one[:blk_i] + tail[1], 2)])
    pieces_one = [with_extra(up_one[k], extra) for k in range(n_y)]
    pieces_near = for_x(grad, slice(0, blk_j))
    parts_far, pieces_near, pieces_one[0] = lax.optimization_barrier((parts_far, pieces_near, pieces_one[0]))
    far = sum(part.astype(F32) for part in parts_far)
    far = with_extra(
        far[:part_rows].astype(BF16), extra_rows([(v, 2) for v in read_rows(far[part_rows:], (2, 2))])
    )
    far = swap(far, "zh").astype(F32)
    near = collect(pieces_near, "x")

    up_one = collect(pieces_one, "y")
    cross_one, mean_up_one = read_rows(up_one[n_x * rows :], (2, 2))
    delta_one = delta(
        norm_one[: n_x * rows, :blk_i], up_one[: n_x * rows], cross_one, mean_up_one, rstd_one
    )
    delta_one = trade_back(delta_one.reshape(n_x, rows, blk_i), "x")
    near, delta_one = lax.optimization_barrier((near, delta_one))

    up_two = near[:part_rows] + far[:part_rows]
    cross_two, mean_up_two = (
        a + b for a, b in zip(read_rows(near[part_rows:], (2, 2)), read_rows(far[part_rows:], (2, 2)))
    )
    normal = norm_two.reshape(n_y, n_x, rows, tile_j)[:, 0, :, :blk_j].reshape(part_rows, blk_j)
    delta_two = delta(normal, up_two, cross_two, mean_up_two, rstd_two)
    delta_two = rotate(gather_columns(delta_two, "y"), ((n_y - at_y) % n_y) * blk_j)

    def input_grad(value):
        far = dot(value, far_keep, 1, 1) + swap(dot(value, far_give, 1, 1).astype(BF16), "c").astype(F32)
        far = swap(far.astype(BF16), "zh").astype(F32)
        near = dot(value, near_keep, 1, 1) + swap(dot(value, near_give, 1, 1).astype(BF16), "c").astype(F32)
        return (near + far).astype(BF16)

    grad_two = input_grad(delta_two)
    return input_grad(delta_one), grad_two


def solution(mesh):
    fine = Mesh(mesh.devices.reshape(4, 4, 4, 2, 2), ("zl", "y", "x", "zh", "c"))
    spec = P(("zl", "y", "x"), ("zh", "c"))
    return jax.shard_map(
        local,
        mesh=fine,
        in_specs=(spec, spec, P(None, ("zh", "c"))),
        out_specs=(spec, spec),
        check_vma=False,
    )
```

```python
import jax
import jax.numpy as jnp
from jax import lax
from jax.sharding import Mesh, PartitionSpec as P

OFF_WEIGHT = 0.0125
EPSILON = 1e-05
F32 = jnp.float32
BF16 = jnp.bfloat16
SWAP = [(0, 1), (1, 0)]
EXTRA = 16


def dot(left, right, left_dim, right_dim):
    return lax.dot_general(
        left, right, (((left_dim,), (right_dim,)), ((), ())), preferred_element_type=F32
    )


def swap(value, axis):
    return lax.ppermute(value, axis, SWAP)


def gather_zl(value):
    count = lax.axis_size("zl")
    return lax.all_to_all(
        jnp.broadcast_to(value[None], (count,) + value.shape), "zl", 0, 0, tiled=True
    )


def shift(value, axis, step):
    count = lax.axis_size(axis)
    return lax.ppermute(value, axis, [(i, (i + step) % count) for i in range(count)])


def small_gather_zl(value):
    return [value] + [shift(value, "zl", step) for step in range(1, lax.axis_size("zl"))]


def rotate(value, start):
    return lax.dynamic_slice_in_dim(jnp.concatenate([value, value], axis=1), start, value.shape[1], 1)


def scatter_columns(rotated, axis):
    count = lax.axis_size(axis)
    blocks = jnp.split(rotated, count, axis=1)
    return jnp.concatenate([blocks[0]] + [shift(blocks[k], axis, k) for k in range(1, count)], axis=0)


def gather_columns(stacked, axis):
    count = lax.axis_size(axis)
    blocks = jnp.split(stacked, count, axis=0)
    return jnp.concatenate([blocks[0]] + [shift(blocks[k], axis, -k) for k in range(1, count)], axis=1)


def trade(slots, axis):
    return lax.all_to_all(slots, axis, 0, 0, tiled=True)


def own_order(chunks, axis):
    count = lax.axis_size(axis)
    chunks = chunks[::-1]
    return lax.dynamic_slice_in_dim(
        jnp.concatenate([chunks, chunks]), count - 1 - lax.axis_index(axis), count, 0
    )


def trade_back(chunks, axis):
    out = trade(own_order(chunks, axis), axis)
    return jnp.concatenate([out[k] for k in range(out.shape[0])], axis=1)


def spread(value, axis):
    return [value] + [shift(value, axis, k) for k in range(1, lax.axis_size(axis))]


def collect(pieces, axis):
    return sum(
        (piece if k == 0 else shift(piece, axis, -k)).astype(F32) for k, piece in enumerate(pieces)
    )


def combine(means, squares, rows):
    mean = sum(means) / len(means)
    return mean, sum(squares) + rows * sum((m - mean) ** 2 for m in means)


def moments(values):
    rows = values.shape[0]
    wide = values.astype(F32)
    mean = jnp.sum(wide, axis=0) / rows
    square = jnp.sum((wide - mean) ** 2, axis=0)
    parts = small_gather_zl(jnp.stack([mean, square]))
    return combine([p[0] for p in parts], [p[1] for p in parts], rows)


def split(vector, pieces):
    out = []
    for _ in range(pieces):
        high = lax.reduce_precision(vector, 8, 7)
        out.append(high.astype(BF16))
        vector = vector - high
    return out


def extra_rows(vectors):
    rows = [piece for vector, pieces in vectors for piece in split(vector, pieces)]
    stacked = jnp.stack(rows)
    return jnp.pad(stacked, ((0, EXTRA - len(rows)),) + ((0, 0),) * (stacked.ndim - 1))


def read_rows(rows, pieces):
    out, at = [], 0
    for count in pieces:
        out.append(sum(rows[at + k] for k in range(count)))
        at += count
    return out


def local(view_one, view_two, proj_weight):
    rows, width = view_one.shape
    n_zl, n_y, n_x = lax.axis_size("zl"), lax.axis_size("y"), lax.axis_size("x")
    n_plane = n_y * n_x
    total_rows = rows * n_zl * n_plane
    blk_i, blk_j = width // n_x, width // n_y
    core = lax.axis_index("c")
    zh = lax.axis_index("zh")

    at_x, at_y = lax.axis_index("x"), lax.axis_index("y")
    rotated_two = rotate(view_two, at_y * blk_j)
    crossed = swap(rotated_two, "zh")
    rotated_one = rotate(view_one, at_x * blk_i)
    plane_rows = n_plane * rows

    def plane_of_two(rotated):
        parts = spread(scatter_columns(rotated, "y"), "x")
        parts = [part.reshape(n_y, 1, rows, blk_j) for part in parts]
        return jnp.concatenate(parts, axis=1).reshape(plane_rows, blk_j)

    own_one = jnp.concatenate(spread(scatter_columns(rotated_one, "x"), "y"), axis=0)
    own = jnp.concatenate([own_one, plane_of_two(rotated_two)], axis=1)
    far_two = plane_of_two(crossed)

    def normalize(values, mean, rstd):
        return ((values.astype(F32) - mean) * rstd).astype(BF16)

    mean, square = moments(own)
    rstd = lax.rsqrt(square / total_rows + EPSILON)
    norm_own = normalize(own, mean, rstd)
    sums_own = jnp.sum(norm_own.astype(F32), axis=0)
    far_stats = swap(jnp.stack([mean[blk_i:], rstd[blk_i:], sums_own[blk_i:]]), "zh")
    sums_one = jnp.concatenate([sums_own[:blk_i], swap(sums_own[:blk_i], "c")])
    sums_two = jnp.concatenate([sums_own[blk_i:], far_stats[2]])
    norm_one = jnp.concatenate([norm_own[:, :blk_i], swap(norm_own[:, :blk_i], "c")], axis=1)
    norm_two = jnp.concatenate([norm_own[:, blk_i:], normalize(far_two, far_stats[0], far_stats[1])], axis=1)
    rstd_one, rstd_two = rstd[:blk_i], rstd[blk_i:]

    tile_i, tile_j = norm_one.shape[1], norm_two.shape[1]
    part = dot(norm_one, norm_two, 0, 0).astype(BF16).reshape(n_zl, tile_i // n_zl, tile_j)
    sums = extra_rows([(sums_one, 2), (sums_two, 2)])
    part = jnp.concatenate([part, jnp.broadcast_to(sums[None], (n_zl,) + sums.shape)], axis=1)
    part = jnp.sum(lax.all_to_all(part, "zl", 0, 0, tiled=True).astype(F32), axis=0)
    slice_i = tile_i // n_zl
    mu_one, mu_two = (v / total_rows for v in read_rows(part[slice_i:], (2, 2)))
    corr = part[:slice_i] / total_rows
    on_diag = lax.axis_index("x") == lax.axis_index("y")

    def diagonal(height, first):
        row_ids = first + lax.broadcasted_iota(jnp.int32, (height, tile_j), 0)
        col_ids = lax.broadcasted_iota(jnp.int32, (height, tile_j), 1)
        return (row_ids == col_ids) & (row_ids < blk_i) & on_diag

    grad = jnp.where(
        diagonal(slice_i, lax.axis_index("zl") * slice_i),
        -2.0 * (1.0 - corr),
        2.0 * OFF_WEIGHT * corr,
    ).astype(BF16)
    grad = gather_zl(grad).reshape(tile_i, tile_j)

    weight = proj_weight.reshape(2, 2, width, width)

    def block(half, member):
        return lax.dynamic_slice(weight, (half, member, 0, 0), (1, 1, width, width)).reshape(width, width)

    far_give, far_keep = block(1 - zh, 1 - core), block(1 - zh, core)
    near_give, near_keep = block(zh, 1 - core), block(zh, core)
    blocks = (far_give, far_keep, near_give, near_keep)
    (far_give, far_keep, near_give, near_keep), grad = lax.optimization_barrier((blocks, grad))

    def products(grad):
        wide = grad.astype(F32)
        return wide, wide * jnp.where(diagonal(tile_i, 0), 1.0 + 0.5 * wide, wide / (2.0 * OFF_WEIGHT))

    def delta(normal, upstream, cross, mean_up, rstd):
        return (rstd * (upstream - mean_up - normal.astype(F32) * cross)).astype(BF16)

    def with_extra(piece, extra):
        return jnp.concatenate([piece.reshape(-1, piece.shape[-1]), extra], axis=0)

    part_rows = n_y * rows

    def for_x(grad, columns):
        wide, product = products(grad)
        cross, mean_up = jnp.sum(product, axis=0), jnp.sum(wide * mu_one[:, None], axis=0)
        extra = extra_rows([(cross[columns], 2), (mean_up[columns], 2)])
        upstream = dot(norm_one, grad[:, columns], 1, 0).astype(BF16).reshape(n_y, n_x, rows, -1)
        return [with_extra(upstream[:, k], extra) for k in range(n_x)]

    pieces_far, grad = lax.optimization_barrier((for_x(grad, slice(blk_j, None)), grad))
    parts_far = [piece if k == 0 else shift(piece, "x", -k) for k, piece in enumerate(pieces_far)]

    wide, product = products(grad)
    cross_one, mean_up_one = jnp.sum(product, axis=1), jnp.sum(wide * mu_two[None, :], axis=1)
    other = with_extra(
        dot(norm_two, grad[blk_i:], 1, 1).astype(BF16),
        extra_rows([(cross_one[blk_i:], 2), (mean_up_one[blk_i:], 2)]),
    )
    other, grad = lax.optimization_barrier((other, grad))
    other = swap(other, "c").astype(F32)
    up_one = (dot(norm_two, grad[:blk_i], 1, 1) + other[:plane_rows]).astype(BF16)
    up_one = up_one.reshape(n_y, n_x * rows, blk_i)
    tail = read_rows(other[plane_rows:], (2, 2))
    extra = extra_rows([(cross_one[:blk_i] + tail[0], 2), (mean_up_one[:blk_i] + tail[1], 2)])
    slots_one = jnp.stack([with_extra(up_one[k], extra) for k in range(n_y)])
    pieces_near = for_x(grad, slice(0, blk_j))
    got_one = trade(own_order(slots_one, "y"), "y")
    parts_far, pieces_near = lax.optimization_barrier((parts_far, pieces_near))
    far = sum(part.astype(F32) for part in parts_far)
    far = with_extra(
        far[:part_rows].astype(BF16), extra_rows([(v, 2) for v in read_rows(far[part_rows:], (2, 2))])
    )
    far = swap(far, "zh").astype(F32)
    near = collect(pieces_near, "x")

    up_one = jnp.sum(got_one.astype(F32), axis=0)
    cross_one, mean_up_one = read_rows(up_one[n_x * rows :], (2, 2))
    delta_one = delta(
        norm_one[: n_x * rows, :blk_i], up_one[: n_x * rows], cross_one, mean_up_one, rstd_one
    )
    delta_one = trade_back(delta_one.reshape(n_x, rows, blk_i), "x")

    up_two = near[:part_rows] + far[:part_rows]
    cross_two, mean_up_two = (
        a + b for a, b in zip(read_rows(near[part_rows:], (2, 2)), read_rows(far[part_rows:], (2, 2)))
    )
    normal = norm_two.reshape(n_y, n_x, rows, tile_j)[:, 0, :, :blk_j].reshape(part_rows, blk_j)
    delta_two = delta(normal, up_two, cross_two, mean_up_two, rstd_two)
    delta_two = rotate(gather_columns(delta_two, "y"), ((n_y - at_y) % n_y) * blk_j)

    def input_grad(value):
        far = dot(value, far_keep, 1, 1) + swap(dot(value, far_give, 1, 1).astype(BF16), "c").astype(F32)
        far = swap(far.astype(BF16), "zh").astype(F32)
        near = dot(value, near_keep, 1, 1) + swap(dot(value, near_give, 1, 1).astype(BF16), "c").astype(F32)
        return (near + far).astype(BF16)

    grad_two = input_grad(delta_two)
    return input_grad(delta_one), grad_two


def solution(mesh):
    fine = Mesh(mesh.devices.reshape(4, 4, 4, 2, 2), ("zl", "y", "x", "zh", "c"))
    spec = P(("zl", "y", "x"), ("zh", "c"))
    return jax.shard_map(
        local,
        mesh=fine,
        in_specs=(spec, spec, P(None, ("zh", "c"))),
        out_specs=(spec, spec),
        check_vma=False,
    )
```

```python
import jax
import jax.numpy as jnp
from jax import lax
from jax.sharding import Mesh, PartitionSpec as P

OFF_WEIGHT = 0.0125
EPSILON = 1e-05
F32 = jnp.float32
BF16 = jnp.bfloat16
SWAP = [(0, 1), (1, 0)]
EXTRA = 16


def dot(left, right, left_dim, right_dim):
    return lax.dot_general(
        left, right, (((left_dim,), (right_dim,)), ((), ())), preferred_element_type=F32
    )


def swap(value, axis):
    return lax.ppermute(value, axis, SWAP)


def gather_zl(value):
    count = lax.axis_size("zl")
    return lax.all_to_all(
        jnp.broadcast_to(value[None], (count,) + value.shape), "zl", 0, 0, tiled=True
    )


def shift(value, axis, step):
    count = lax.axis_size(axis)
    return lax.ppermute(value, axis, [(i, (i + step) % count) for i in range(count)])


def small_gather_zl(value):
    return [value] + [shift(value, "zl", step) for step in range(1, lax.axis_size("zl"))]


def rotate(value, start):
    return lax.dynamic_slice_in_dim(jnp.concatenate([value, value], axis=1), start, value.shape[1], 1)


def scatter_columns(rotated, axis):
    count = lax.axis_size(axis)
    blocks = jnp.split(rotated, count, axis=1)
    return jnp.concatenate([blocks[0]] + [shift(blocks[k], axis, k) for k in range(1, count)], axis=0)


def gather_columns(stacked, axis):
    count = lax.axis_size(axis)
    blocks = jnp.split(stacked, count, axis=0)
    return jnp.concatenate([blocks[0]] + [shift(blocks[k], axis, -k) for k in range(1, count)], axis=1)


def trade_back(chunks, axis):
    count = lax.axis_size(axis)
    chunks = chunks[::-1]
    slots = lax.dynamic_slice_in_dim(
        jnp.concatenate([chunks, chunks]), count - 1 - lax.axis_index(axis), count, 0
    )
    out = lax.all_to_all(slots, axis, 0, 0, tiled=True)
    return jnp.concatenate([out[k] for k in range(count)], axis=1)


def spread(value, axis):
    return [value] + [shift(value, axis, k) for k in range(1, lax.axis_size(axis))]


def collect(pieces, axis):
    return sum(
        (piece if k == 0 else shift(piece, axis, -k)).astype(F32) for k, piece in enumerate(pieces)
    )


def combine(means, squares, rows):
    mean = sum(means) / len(means)
    return mean, sum(squares) + rows * sum((m - mean) ** 2 for m in means)


def moments(values):
    rows = values.shape[0]
    wide = values.astype(F32)
    mean = jnp.sum(wide, axis=0) / rows
    square = jnp.sum((wide - mean) ** 2, axis=0)
    parts = small_gather_zl(jnp.stack([mean, square]))
    return combine([p[0] for p in parts], [p[1] for p in parts], rows)


def split(vector, pieces):
    out = []
    for _ in range(pieces):
        high = lax.reduce_precision(vector, 8, 7)
        out.append(high.astype(BF16))
        vector = vector - high
    return out


def extra_rows(vectors):
    rows = [piece for vector, pieces in vectors for piece in split(vector, pieces)]
    stacked = jnp.stack(rows)
    return jnp.pad(stacked, ((0, EXTRA - len(rows)),) + ((0, 0),) * (stacked.ndim - 1))


def read_rows(rows, pieces):
    out, at = [], 0
    for count in pieces:
        out.append(sum(rows[at + k] for k in range(count)))
        at += count
    return out


def local(view_one, view_two, proj_weight):
    rows, width = view_one.shape
    n_zl, n_y, n_x = lax.axis_size("zl"), lax.axis_size("y"), lax.axis_size("x")
    n_plane = n_y * n_x
    total_rows = rows * n_zl * n_plane
    blk_i, blk_j = width // n_x, width // n_y
    core = lax.axis_index("c")
    zh = lax.axis_index("zh")

    at_x, at_y = lax.axis_index("x"), lax.axis_index("y")
    rotated_two = rotate(view_two, at_y * blk_j)
    crossed = swap(rotated_two, "zh")
    rotated_one = rotate(view_one, at_x * blk_i)
    plane_rows = n_plane * rows

    def plane_of_two(rotated):
        parts = spread(scatter_columns(rotated, "y"), "x")
        parts = [part.reshape(n_y, 1, rows, blk_j) for part in parts]
        return jnp.concatenate(parts, axis=1).reshape(plane_rows, blk_j)

    own_one = jnp.concatenate(spread(scatter_columns(rotated_one, "x"), "y"), axis=0)
    own = jnp.concatenate([own_one, plane_of_two(rotated_two)], axis=1)
    far_two = plane_of_two(crossed)

    def normalize(values, mean, rstd):
        return ((values.astype(F32) - mean) * rstd).astype(BF16)

    mean, square = moments(own)
    rstd = lax.rsqrt(square / total_rows + EPSILON)
    norm_own = normalize(own, mean, rstd)
    sums_own = jnp.sum(norm_own.astype(F32), axis=0)
    far_stats = swap(jnp.stack([mean[blk_i:], rstd[blk_i:], sums_own[blk_i:]]), "zh")
    sums_one = jnp.concatenate([sums_own[:blk_i], swap(sums_own[:blk_i], "c")])
    sums_two = jnp.concatenate([sums_own[blk_i:], far_stats[2]])
    norm_one = jnp.concatenate([norm_own[:, :blk_i], swap(norm_own[:, :blk_i], "c")], axis=1)
    norm_two = jnp.concatenate([norm_own[:, blk_i:], normalize(far_two, far_stats[0], far_stats[1])], axis=1)
    rstd_one, rstd_two = rstd[:blk_i], rstd[blk_i:]

    tile_i, tile_j = norm_one.shape[1], norm_two.shape[1]
    part = dot(norm_one, norm_two, 0, 0).astype(BF16).reshape(n_zl, tile_i // n_zl, tile_j)
    sums = extra_rows([(sums_one, 2), (sums_two, 2)])
    part = jnp.concatenate([part, jnp.broadcast_to(sums[None], (n_zl,) + sums.shape)], axis=1)
    part = jnp.sum(lax.all_to_all(part, "zl", 0, 0, tiled=True).astype(F32), axis=0)
    slice_i = tile_i // n_zl
    mu_one, mu_two = (v / total_rows for v in read_rows(part[slice_i:], (2, 2)))
    corr = part[:slice_i] / total_rows
    on_diag = lax.axis_index("x") == lax.axis_index("y")

    def diagonal(height, first):
        row_ids = first + lax.broadcasted_iota(jnp.int32, (height, tile_j), 0)
        col_ids = lax.broadcasted_iota(jnp.int32, (height, tile_j), 1)
        return (row_ids == col_ids) & (row_ids < blk_i) & on_diag

    grad = jnp.where(
        diagonal(slice_i, lax.axis_index("zl") * slice_i),
        -2.0 * (1.0 - corr),
        2.0 * OFF_WEIGHT * corr,
    ).astype(BF16)
    grad = gather_zl(grad).reshape(tile_i, tile_j)

    weight = proj_weight.reshape(2, 2, width, width)

    def block(half, member):
        return lax.dynamic_slice(weight, (half, member, 0, 0), (1, 1, width, width)).reshape(width, width)

    far_give, far_keep = block(1 - zh, 1 - core), block(1 - zh, core)
    near_give, near_keep = block(zh, 1 - core), block(zh, core)
    blocks = (far_give, far_keep, near_give, near_keep)
    (far_give, far_keep, near_give, near_keep), grad = lax.optimization_barrier((blocks, grad))

    def products(grad):
        wide = grad.astype(F32)
        return wide, wide * jnp.where(diagonal(tile_i, 0), 1.0 + 0.5 * wide, wide / (2.0 * OFF_WEIGHT))

    def delta(normal, upstream, cross, mean_up, rstd):
        return (rstd * (upstream - mean_up - normal.astype(F32) * cross)).astype(BF16)

    def with_extra(piece, extra):
        return jnp.concatenate([piece.reshape(-1, piece.shape[-1]), extra], axis=0)

    wide, product = products(grad)
    cross_one, mean_up_one = jnp.sum(product, axis=1), jnp.sum(wide * mu_two[None, :], axis=1)
    up_one = dot(norm_two, grad, 1, 1)
    other = with_extra(
        up_one[:, blk_i:].astype(BF16), extra_rows([(cross_one[blk_i:], 2), (mean_up_one[blk_i:], 2)])
    )
    other, grad = lax.optimization_barrier((other, grad))
    other = swap(other, "c")

    wide, product = products(grad)
    cross_two, mean_up_two = jnp.sum(product, axis=0), jnp.sum(wide * mu_one[:, None], axis=0)
    up_two = dot(norm_one, grad, 1, 0).astype(BF16).reshape(n_y, n_x, rows, tile_j)

    def for_x(columns):
        extra = extra_rows([(cross_two[columns], 2), (mean_up_two[columns], 2)])
        return [with_extra(up_two[:, k, :, columns], extra) for k in range(n_x)]

    pieces_far, pieces_near = for_x(slice(blk_j, None)), for_x(slice(0, blk_j))
    other, pieces_far, pieces_near = lax.optimization_barrier((other, pieces_far, pieces_near))

    other = other.astype(F32)
    up_one = (up_one[:, :blk_i] + other[:plane_rows]).astype(BF16).reshape(n_y, n_x * rows, blk_i)
    tail = read_rows(other[plane_rows:], (2, 2))
    extra = extra_rows([(cross_one[:blk_i] + tail[0], 2), (mean_up_one[:blk_i] + tail[1], 2)])
    pieces_one = [with_extra(up_one[k], extra) for k in range(n_y)]
    pieces_one, pieces_far = lax.optimization_barrier((pieces_one, pieces_far))

    part_rows = n_y * rows
    far = collect(pieces_far, "x")
    far = with_extra(
        far[:part_rows].astype(BF16), extra_rows([(v, 2) for v in read_rows(far[part_rows:], (2, 2))])
    )
    far, pieces_near = lax.optimization_barrier((far, pieces_near))
    far = swap(far, "zh").astype(F32)

    up_one = collect(pieces_one, "y")
    cross_one, mean_up_one = read_rows(up_one[n_x * rows :], (2, 2))
    delta_one = delta(
        norm_one[: n_x * rows, :blk_i], up_one[: n_x * rows], cross_one, mean_up_one, rstd_one
    )
    delta_one = trade_back(delta_one.reshape(n_x, rows, blk_i), "x")

    near = collect(pieces_near, "x")
    near, delta_one = lax.optimization_barrier((near, delta_one))
    up_two = near[:part_rows] + far[:part_rows]
    cross_two, mean_up_two = (
        a + b for a, b in zip(read_rows(near[part_rows:], (2, 2)), read_rows(far[part_rows:], (2, 2)))
    )
    normal = norm_two.reshape(n_y, n_x, rows, tile_j)[:, 0, :, :blk_j].reshape(part_rows, blk_j)
    delta_two = delta(normal, up_two, cross_two, mean_up_two, rstd_two)
    delta_two = rotate(gather_columns(delta_two, "y"), ((n_y - at_y) % n_y) * blk_j)

    def sum_cores(value, keep, give):
        return dot(value, keep, 1, 1) + swap(dot(value, give, 1, 1).astype(BF16), "c").astype(F32)

    far_one = swap(sum_cores(delta_one, far_keep, far_give).astype(BF16), "zh")
    near_one = sum_cores(delta_one, near_keep, near_give)
    far_two = sum_cores(delta_two, far_keep, far_give).astype(BF16)
    far_one, far_two = lax.optimization_barrier((far_one, far_two))
    far_two = swap(far_two, "zh")
    near_two = sum_cores(delta_two, near_keep, near_give)
    return (
        (near_one + far_one.astype(F32)).astype(BF16),
        (near_two + far_two.astype(F32)).astype(BF16),
    )


def solution(mesh):
    fine = Mesh(mesh.devices.reshape(4, 4, 4, 2, 2), ("zl", "y", "x", "zh", "c"))
    spec = P(("zl", "y", "x"), ("zh", "c"))
    return jax.shard_map(
        local,
        mesh=fine,
        in_specs=(spec, spec, P(None, ("zh", "c"))),
        out_specs=(spec, spec),
        check_vma=False,
    )
```

```python
import jax
import jax.numpy as jnp
from jax import lax
from jax.sharding import Mesh, PartitionSpec as P

OFF_WEIGHT = 0.0125
EPSILON = 1e-05
F32 = jnp.float32
BF16 = jnp.bfloat16
SWAP = [(0, 1), (1, 0)]
EXTRA = 16


def dot(left, right, left_dim, right_dim):
    return lax.dot_general(
        left, right, (((left_dim,), (right_dim,)), ((), ())), preferred_element_type=F32
    )


def swap(value, axis):
    return lax.ppermute(value, axis, SWAP)


def gather_zl(value):
    count = lax.axis_size("zl")
    return lax.all_to_all(
        jnp.broadcast_to(value[None], (count,) + value.shape), "zl", 0, 0, tiled=True
    )


def shift(value, axis, step):
    count = lax.axis_size(axis)
    return lax.ppermute(value, axis, [(i, (i + step) % count) for i in range(count)])


def small_gather_zl(value):
    return [value] + [shift(value, "zl", step) for step in range(1, lax.axis_size("zl"))]


def rotate(value, start):
    return lax.dynamic_slice_in_dim(jnp.concatenate([value, value], axis=1), start, value.shape[1], 1)


def scatter_columns(rotated, axis):
    count = lax.axis_size(axis)
    blocks = jnp.split(rotated, count, axis=1)
    return jnp.concatenate([blocks[0]] + [shift(blocks[k], axis, k) for k in range(1, count)], axis=0)


def gather_columns(stacked, axis):
    count = lax.axis_size(axis)
    blocks = jnp.split(stacked, count, axis=0)
    return jnp.concatenate([blocks[0]] + [shift(blocks[k], axis, -k) for k in range(1, count)], axis=1)


def trade_back(chunks, axis):
    count = lax.axis_size(axis)
    chunks = chunks[::-1]
    slots = lax.dynamic_slice_in_dim(
        jnp.concatenate([chunks, chunks]), count - 1 - lax.axis_index(axis), count, 0
    )
    out = lax.all_to_all(slots, axis, 0, 0, tiled=True)
    return jnp.concatenate([out[k] for k in range(count)], axis=1)


def spread(value, axis):
    return [value] + [shift(value, axis, k) for k in range(1, lax.axis_size(axis))]


def collect(pieces, axis):
    return sum(
        (piece if k == 0 else shift(piece, axis, -k)).astype(F32) for k, piece in enumerate(pieces)
    )


def combine(means, squares, rows):
    mean = sum(means) / len(means)
    return mean, sum(squares) + rows * sum((m - mean) ** 2 for m in means)


def moments(values):
    rows = values.shape[0]
    wide = values.astype(F32)
    mean = jnp.sum(wide, axis=0) / rows
    square = jnp.sum((wide - mean) ** 2, axis=0)
    parts = small_gather_zl(jnp.stack([mean, square]))
    return combine([p[0] for p in parts], [p[1] for p in parts], rows)


def split(vector, pieces):
    out = []
    for _ in range(pieces):
        high = lax.reduce_precision(vector, 8, 7)
        out.append(high.astype(BF16))
        vector = vector - high
    return out


def extra_rows(vectors):
    rows = [piece for vector, pieces in vectors for piece in split(vector, pieces)]
    stacked = jnp.stack(rows)
    return jnp.pad(stacked, ((0, EXTRA - len(rows)),) + ((0, 0),) * (stacked.ndim - 1))


def read_rows(rows, pieces):
    out, at = [], 0
    for count in pieces:
        out.append(sum(rows[at + k] for k in range(count)))
        at += count
    return out


def local(view_one, view_two, proj_weight):
    rows, width = view_one.shape
    n_zl, n_y, n_x = lax.axis_size("zl"), lax.axis_size("y"), lax.axis_size("x")
    n_plane = n_y * n_x
    total_rows = rows * n_zl * n_plane
    blk_i, blk_j = width // n_x, width // n_y
    core = lax.axis_index("c")
    zh = lax.axis_index("zh")

    at_x, at_y = lax.axis_index("x"), lax.axis_index("y")
    rotated_two = rotate(view_two, at_y * blk_j)
    crossed = swap(rotated_two, "zh")
    rotated_one = rotate(view_one, at_x * blk_i)
    plane_rows = n_plane * rows

    def plane_of_two(rotated):
        parts = spread(scatter_columns(rotated, "y"), "x")
        parts = [part.reshape(n_y, 1, rows, blk_j) for part in parts]
        return jnp.concatenate(parts, axis=1).reshape(plane_rows, blk_j)

    own_one = jnp.concatenate(spread(scatter_columns(rotated_one, "x"), "y"), axis=0)
    own = jnp.concatenate([own_one, plane_of_two(rotated_two)], axis=1)
    far_two = plane_of_two(crossed)

    def normalize(values, mean, rstd):
        return ((values.astype(F32) - mean) * rstd).astype(BF16)

    mean, square = moments(own)
    rstd = lax.rsqrt(square / total_rows + EPSILON)
    norm_own = normalize(own, mean, rstd)
    sums_own = jnp.sum(norm_own.astype(F32), axis=0)
    far_stats = swap(jnp.stack([mean[blk_i:], rstd[blk_i:], sums_own[blk_i:]]), "zh")
    sums_one = jnp.concatenate([sums_own[:blk_i], swap(sums_own[:blk_i], "c")])
    sums_two = jnp.concatenate([sums_own[blk_i:], far_stats[2]])
    norm_one = jnp.concatenate([norm_own[:, :blk_i], swap(norm_own[:, :blk_i], "c")], axis=1)
    norm_two = jnp.concatenate([norm_own[:, blk_i:], normalize(far_two, far_stats[0], far_stats[1])], axis=1)
    rstd_one, rstd_two = rstd[:blk_i], rstd[blk_i:]

    tile_i, tile_j = norm_one.shape[1], norm_two.shape[1]
    part = dot(norm_one, norm_two, 0, 0).astype(BF16).reshape(n_zl, tile_i // n_zl, tile_j)
    sums = extra_rows([(sums_one, 2), (sums_two, 2)])
    part = jnp.concatenate([part, jnp.broadcast_to(sums[None], (n_zl,) + sums.shape)], axis=1)
    part = jnp.sum(lax.all_to_all(part, "zl", 0, 0, tiled=True).astype(F32), axis=0)
    slice_i = tile_i // n_zl
    mu_one, mu_two = (v / total_rows for v in read_rows(part[slice_i:], (2, 2)))
    corr = part[:slice_i] / total_rows
    on_diag = lax.axis_index("x") == lax.axis_index("y")

    def diagonal(height, first):
        row_ids = first + lax.broadcasted_iota(jnp.int32, (height, tile_j), 0)
        col_ids = lax.broadcasted_iota(jnp.int32, (height, tile_j), 1)
        return (row_ids == col_ids) & (row_ids < blk_i) & on_diag

    grad = jnp.where(
        diagonal(slice_i, lax.axis_index("zl") * slice_i),
        -2.0 * (1.0 - corr),
        2.0 * OFF_WEIGHT * corr,
    ).astype(BF16)
    grad = gather_zl(grad).reshape(tile_i, tile_j)

    weight = proj_weight.reshape(2, 2, width, width)

    def block(half, member):
        return lax.dynamic_slice(weight, (half, member, 0, 0), (1, 1, width, width)).reshape(width, width)

    far_give, far_keep = block(1 - zh, 1 - core), block(1 - zh, core)
    near_give, near_keep = block(zh, 1 - core), block(zh, core)
    blocks = (far_give, far_keep, near_give, near_keep)
    (far_give, far_keep, near_give, near_keep), grad = lax.optimization_barrier((blocks, grad))

    def products(grad):
        wide = grad.astype(F32)
        return wide, wide * jnp.where(diagonal(tile_i, 0), 1.0 + 0.5 * wide, wide / (2.0 * OFF_WEIGHT))

    def delta(normal, upstream, cross, mean_up, rstd):
        return (rstd * (upstream - mean_up - normal.astype(F32) * cross)).astype(BF16)

    def with_extra(piece, extra):
        return jnp.concatenate([piece.reshape(-1, piece.shape[-1]), extra], axis=0)

    wide, product = products(grad)
    cross_one, mean_up_one = jnp.sum(product, axis=1), jnp.sum(wide * mu_two[None, :], axis=1)
    up_one = dot(norm_two, grad, 1, 1)
    other = with_extra(
        up_one[:, blk_i:].astype(BF16), extra_rows([(cross_one[blk_i:], 2), (mean_up_one[blk_i:], 2)])
    )
    other, grad = lax.optimization_barrier((other, grad))
    other = swap(other, "c")

    wide, product = products(grad)
    cross_two, mean_up_two = jnp.sum(product, axis=0), jnp.sum(wide * mu_one[:, None], axis=0)
    up_two = dot(norm_one, grad, 1, 0).astype(BF16).reshape(n_y, n_x, rows, tile_j)

    def for_x(columns):
        extra = extra_rows([(cross_two[columns], 2), (mean_up_two[columns], 2)])
        return [with_extra(up_two[:, k, :, columns], extra) for k in range(n_x)]

    pieces_far, pieces_near = for_x(slice(blk_j, None)), for_x(slice(0, blk_j))
    other, pieces_far, pieces_near = lax.optimization_barrier((other, pieces_far, pieces_near))

    other = other.astype(F32)
    up_one = (up_one[:, :blk_i] + other[:plane_rows]).astype(BF16).reshape(n_y, n_x * rows, blk_i)
    tail = read_rows(other[plane_rows:], (2, 2))
    extra = extra_rows([(cross_one[:blk_i] + tail[0], 2), (mean_up_one[:blk_i] + tail[1], 2)])
    pieces_one = [with_extra(up_one[k], extra) for k in range(n_y)]
    pieces_one, pieces_far = lax.optimization_barrier((pieces_one, pieces_far))

    part_rows = n_y * rows
    far = collect(pieces_far, "x")
    far = with_extra(
        far[:part_rows].astype(BF16), extra_rows([(v, 2) for v in read_rows(far[part_rows:], (2, 2))])
    )
    far, pieces_near = lax.optimization_barrier((far, pieces_near))
    far = swap(far, "zh").astype(F32)

    up_one = collect(pieces_one, "y")
    cross_one, mean_up_one = read_rows(up_one[n_x * rows :], (2, 2))
    delta_one = delta(
        norm_one[: n_x * rows, :blk_i], up_one[: n_x * rows], cross_one, mean_up_one, rstd_one
    )
    delta_one = trade_back(delta_one.reshape(n_x, rows, blk_i), "x")

    near = collect(pieces_near, "x")
    up_two = near[:part_rows] + far[:part_rows]
    cross_two, mean_up_two = (
        a + b for a, b in zip(read_rows(near[part_rows:], (2, 2)), read_rows(far[part_rows:], (2, 2)))
    )
    normal = norm_two.reshape(n_y, n_x, rows, tile_j)[:, 0, :, :blk_j].reshape(part_rows, blk_j)
    delta_two = delta(normal, up_two, cross_two, mean_up_two, rstd_two)
    delta_two = rotate(gather_columns(delta_two, "y"), ((n_y - at_y) % n_y) * blk_j)

    def sum_cores(value, keep, give):
        return dot(value, keep, 1, 1) + swap(dot(value, give, 1, 1).astype(BF16), "c").astype(F32)

    far_one = swap(sum_cores(delta_one, far_keep, far_give).astype(BF16), "zh")
    near_one = sum_cores(delta_one, near_keep, near_give)
    far_two = sum_cores(delta_two, far_keep, far_give).astype(BF16)
    far_one, far_two = lax.optimization_barrier((far_one, far_two))
    far_two = swap(far_two, "zh")
    near_two = sum_cores(delta_two, near_keep, near_give)
    return (
        (near_one + far_one.astype(F32)).astype(BF16),
        (near_two + far_two.astype(F32)).astype(BF16),
    )


def solution(mesh):
    fine = Mesh(mesh.devices.reshape(4, 4, 4, 2, 2), ("zl", "y", "x", "zh", "c"))
    spec = P(("zl", "y", "x"), ("zh", "c"))
    return jax.shard_map(
        local,
        mesh=fine,
        in_specs=(spec, spec, P(None, ("zh", "c"))),
        out_specs=(spec, spec),
        check_vma=False,
    )
```

```python
import jax
import jax.numpy as jnp
from jax import lax
from jax.sharding import Mesh, PartitionSpec as P

OFF_WEIGHT = 0.0125
EPSILON = 1e-05
F32 = jnp.float32
BF16 = jnp.bfloat16
SWAP = [(0, 1), (1, 0)]
EXTRA = 16


def dot(left, right, left_dim, right_dim):
    return lax.dot_general(
        left, right, (((left_dim,), (right_dim,)), ((), ())), preferred_element_type=F32
    )


def swap(value, axis):
    return lax.ppermute(value, axis, SWAP)


def gather_zl(value):
    count = lax.axis_size("zl")
    return lax.all_to_all(
        jnp.broadcast_to(value[None], (count,) + value.shape), "zl", 0, 0, tiled=True
    )


def shift(value, axis, step):
    count = lax.axis_size(axis)
    return lax.ppermute(value, axis, [(i, (i + step) % count) for i in range(count)])


def small_gather_zl(value):
    return [value] + [shift(value, "zl", step) for step in range(1, lax.axis_size("zl"))]


def rotate(value, start):
    return lax.dynamic_slice_in_dim(jnp.concatenate([value, value], axis=1), start, value.shape[1], 1)


def scatter_columns(rotated, axis):
    count = lax.axis_size(axis)
    blocks = jnp.split(rotated, count, axis=1)
    return jnp.concatenate([blocks[0]] + [shift(blocks[k], axis, k) for k in range(1, count)], axis=0)


def gather_columns(stacked, axis):
    count = lax.axis_size(axis)
    blocks = jnp.split(stacked, count, axis=0)
    return jnp.concatenate([blocks[0]] + [shift(blocks[k], axis, -k) for k in range(1, count)], axis=1)


def spread(value, axis):
    return [value] + [shift(value, axis, k) for k in range(1, lax.axis_size(axis))]


def collect(pieces, axis):
    return sum(
        (piece if k == 0 else shift(piece, axis, -k)).astype(F32) for k, piece in enumerate(pieces)
    )


def combine(means, squares, rows):
    mean = sum(means) / len(means)
    return mean, sum(squares) + rows * sum((m - mean) ** 2 for m in means)


def moments(values):
    rows = values.shape[0]
    wide = values.astype(F32)
    mean = jnp.sum(wide, axis=0) / rows
    square = jnp.sum((wide - mean) ** 2, axis=0)
    parts = small_gather_zl(jnp.stack([mean, square]))
    return combine([p[0] for p in parts], [p[1] for p in parts], rows)


def split(vector, pieces):
    out = []
    for _ in range(pieces):
        high = lax.reduce_precision(vector, 8, 7)
        out.append(high.astype(BF16))
        vector = vector - high
    return out


def extra_rows(vectors):
    rows = [piece for vector, pieces in vectors for piece in split(vector, pieces)]
    stacked = jnp.stack(rows)
    return jnp.pad(stacked, ((0, EXTRA - len(rows)),) + ((0, 0),) * (stacked.ndim - 1))


def read_rows(rows, pieces):
    out, at = [], 0
    for count in pieces:
        out.append(sum(rows[at + k] for k in range(count)))
        at += count
    return out


def local(view_one, view_two, proj_weight):
    rows, width = view_one.shape
    n_zl, n_y, n_x = lax.axis_size("zl"), lax.axis_size("y"), lax.axis_size("x")
    n_plane = n_y * n_x
    total_rows = rows * n_zl * n_plane
    blk_i, blk_j = width // n_x, width // n_y
    core = lax.axis_index("c")
    zh = lax.axis_index("zh")

    at_x, at_y = lax.axis_index("x"), lax.axis_index("y")
    rotated_two = rotate(view_two, at_y * blk_j)
    crossed = swap(rotated_two, "zh")
    rotated_one = rotate(view_one, at_x * blk_i)
    plane_rows = n_plane * rows

    def plane_of_two(rotated):
        parts = spread(scatter_columns(rotated, "y"), "x")
        parts = [part.reshape(n_y, 1, rows, blk_j) for part in parts]
        return jnp.concatenate(parts, axis=1).reshape(plane_rows, blk_j)

    own_one = jnp.concatenate(spread(scatter_columns(rotated_one, "x"), "y"), axis=0)
    own = jnp.concatenate([own_one, plane_of_two(rotated_two)], axis=1)
    far_two = plane_of_two(crossed)

    def normalize(values, mean, rstd):
        return ((values.astype(F32) - mean) * rstd).astype(BF16)

    mean, square = moments(own)
    rstd = lax.rsqrt(square / total_rows + EPSILON)
    norm_own = normalize(own, mean, rstd)
    sums_own = jnp.sum(norm_own.astype(F32), axis=0)
    far_stats = swap(jnp.stack([mean[blk_i:], rstd[blk_i:], sums_own[blk_i:]]), "zh")
    sums_one = jnp.concatenate([sums_own[:blk_i], swap(sums_own[:blk_i], "c")])
    sums_two = jnp.concatenate([sums_own[blk_i:], far_stats[2]])
    norm_one = jnp.concatenate([norm_own[:, :blk_i], swap(norm_own[:, :blk_i], "c")], axis=1)
    norm_two = jnp.concatenate([norm_own[:, blk_i:], normalize(far_two, far_stats[0], far_stats[1])], axis=1)
    rstd_one, rstd_two = rstd[:blk_i], rstd[blk_i:]

    tile_i, tile_j = norm_one.shape[1], norm_two.shape[1]
    part = dot(norm_one, norm_two, 0, 0).astype(BF16).reshape(n_zl, tile_i // n_zl, tile_j)
    sums = extra_rows([(sums_one, 2), (sums_two, 2)])
    part = jnp.concatenate([part, jnp.broadcast_to(sums[None], (n_zl,) + sums.shape)], axis=1)
    part = jnp.sum(lax.all_to_all(part, "zl", 0, 0, tiled=True).astype(F32), axis=0)
    slice_i = tile_i // n_zl
    mu_one, mu_two = (v / total_rows for v in read_rows(part[slice_i:], (2, 2)))
    corr = part[:slice_i] / total_rows
    on_diag = lax.axis_index("x") == lax.axis_index("y")

    def diagonal(height, first):
        row_ids = first + lax.broadcasted_iota(jnp.int32, (height, tile_j), 0)
        col_ids = lax.broadcasted_iota(jnp.int32, (height, tile_j), 1)
        return (row_ids == col_ids) & (row_ids < blk_i) & on_diag

    grad = jnp.where(
        diagonal(slice_i, lax.axis_index("zl") * slice_i),
        -2.0 * (1.0 - corr),
        2.0 * OFF_WEIGHT * corr,
    ).astype(BF16)
    grad = gather_zl(grad).reshape(tile_i, tile_j)

    def products(grad):
        wide = grad.astype(F32)
        return wide, wide * jnp.where(diagonal(tile_i, 0), 1.0 + 0.5 * wide, wide / (2.0 * OFF_WEIGHT))

    def delta(normal, upstream, cross, mean_up, rstd):
        return (rstd * (upstream - mean_up - normal.astype(F32) * cross)).astype(BF16)

    def with_extra(piece, extra):
        return jnp.concatenate([piece.reshape(-1, piece.shape[-1]), extra], axis=0)

    wide, product = products(grad)
    cross_one, mean_up_one = jnp.sum(product, axis=1), jnp.sum(wide * mu_two[None, :], axis=1)
    other = with_extra(
        dot(norm_two, grad[blk_i:], 1, 1).astype(BF16),
        extra_rows([(cross_one[blk_i:], 2), (mean_up_one[blk_i:], 2)]),
    )
    other, grad = lax.optimization_barrier((other, grad))
    other = swap(other, "c")

    wide, product = products(grad)
    cross_two, mean_up_two = jnp.sum(product, axis=0), jnp.sum(wide * mu_one[:, None], axis=0)
    up_two = dot(norm_one, grad, 1, 0).astype(BF16).reshape(n_y, n_x, rows, tile_j)

    def for_x(columns):
        extra = extra_rows([(cross_two[columns], 2), (mean_up_two[columns], 2)])
        return [with_extra(up_two[:, k, :, columns], extra) for k in range(n_x)]

    pieces_far, pieces_near = for_x(slice(blk_j, None)), for_x(slice(0, blk_j))
    other, pieces_far, pieces_near = lax.optimization_barrier((other, pieces_far, pieces_near))

    other = other.astype(F32)
    up_one = (dot(norm_two, grad[:blk_i], 1, 1) + other[:plane_rows]).astype(BF16)
    up_one = up_one.reshape(n_y, n_x * rows, blk_i)
    tail = read_rows(other[plane_rows:], (2, 2))
    extra = extra_rows([(cross_one[:blk_i] + tail[0], 2), (mean_up_one[:blk_i] + tail[1], 2)])
    pieces_one = [with_extra(up_one[k], extra) for k in range(n_y)]
    pieces_one, pieces_far = lax.optimization_barrier((pieces_one, pieces_far))

    part_rows = n_y * rows
    far = collect(pieces_far, "x")
    far = with_extra(
        far[:part_rows].astype(BF16), extra_rows([(v, 2) for v in read_rows(far[part_rows:], (2, 2))])
    )
    far, pieces_near = lax.optimization_barrier((far, pieces_near))
    near = collect(pieces_near, "x")
    far = swap(far, "zh").astype(F32)

    up_one = collect(pieces_one, "y")
    cross_one, mean_up_one = read_rows(up_one[n_x * rows :], (2, 2))
    delta_one = delta(
        norm_one[: n_x * rows, :blk_i], up_one[: n_x * rows], cross_one, mean_up_one, rstd_one
    )
    delta_one = rotate(gather_columns(delta_one, "x"), ((n_x - at_x) % n_x) * blk_i)

    up_two = near[:part_rows] + far[:part_rows]
    cross_two, mean_up_two = (
        a + b for a, b in zip(read_rows(near[part_rows:], (2, 2)), read_rows(far[part_rows:], (2, 2)))
    )
    normal = norm_two.reshape(n_y, n_x, rows, tile_j)[:, 0, :, :blk_j].reshape(part_rows, blk_j)
    delta_two = delta(normal, up_two, cross_two, mean_up_two, rstd_two)
    delta_two = rotate(gather_columns(delta_two, "y"), ((n_y - at_y) % n_y) * blk_j)

    weight = proj_weight.reshape(2, 2, width, width)

    def block(half, member):
        return lax.dynamic_slice(weight, (half, member, 0, 0), (1, 1, width, width)).reshape(width, width)

    far_give, far_keep = block(1 - zh, 1 - core), block(1 - zh, core)
    near_give, near_keep = block(zh, 1 - core), block(zh, core)

    def input_grad(value):
        far = dot(value, far_keep, 1, 1) + swap(dot(value, far_give, 1, 1).astype(BF16), "c").astype(F32)
        far = swap(far.astype(BF16), "zh").astype(F32)
        near = dot(value, near_keep, 1, 1) + swap(dot(value, near_give, 1, 1).astype(BF16), "c").astype(F32)
        return (lax.optimization_barrier(near) + far).astype(BF16)

    grad_two = input_grad(delta_two)
    return input_grad(delta_one), grad_two


def solution(mesh):
    fine = Mesh(mesh.devices.reshape(4, 4, 4, 2, 2), ("zl", "y", "x", "zh", "c"))
    spec = P(("zl", "y", "x"), ("zh", "c"))
    return jax.shard_map(
        local,
        mesh=fine,
        in_specs=(spec, spec, P(None, ("zh", "c"))),
        out_specs=(spec, spec),
        check_vma=False,
    )
```

```python
import jax
import jax.numpy as jnp
from jax import lax
from jax.sharding import Mesh, PartitionSpec as P

OFF_WEIGHT = 0.0125
EPSILON = 1e-05
F32 = jnp.float32
BF16 = jnp.bfloat16
SWAP = [(0, 1), (1, 0)]
EXTRA = 16


def dot(left, right, left_dim, right_dim):
    return lax.dot_general(
        left, right, (((left_dim,), (right_dim,)), ((), ())), preferred_element_type=F32
    )


def swap(value, axis):
    return lax.ppermute(value, axis, SWAP)


def gather_zl(value):
    count = lax.axis_size("zl")
    return lax.all_to_all(
        jnp.broadcast_to(value[None], (count,) + value.shape), "zl", 0, 0, tiled=True
    )


def shift(value, axis, step):
    count = lax.axis_size(axis)
    return lax.ppermute(value, axis, [(i, (i + step) % count) for i in range(count)])


def small_gather_zl(value):
    return [value] + [shift(value, "zl", step) for step in range(1, lax.axis_size("zl"))]


def rotate(value, start):
    return lax.dynamic_slice_in_dim(jnp.concatenate([value, value], axis=1), start, value.shape[1], 1)


def scatter_columns(rotated, axis):
    count = lax.axis_size(axis)
    blocks = jnp.split(rotated, count, axis=1)
    return jnp.concatenate([blocks[0]] + [shift(blocks[k], axis, k) for k in range(1, count)], axis=0)


def gather_columns(stacked, axis):
    count = lax.axis_size(axis)
    blocks = jnp.split(stacked, count, axis=0)
    return jnp.concatenate([blocks[0]] + [shift(blocks[k], axis, -k) for k in range(1, count)], axis=1)


def spread(value, axis):
    return [value] + [shift(value, axis, k) for k in range(1, lax.axis_size(axis))]


def collect(pieces, axis):
    return sum(
        (piece if k == 0 else shift(piece, axis, -k)).astype(F32) for k, piece in enumerate(pieces)
    )


def combine(means, squares, rows):
    mean = sum(means) / len(means)
    return mean, sum(squares) + rows * sum((m - mean) ** 2 for m in means)


def moments(values):
    rows = values.shape[0]
    wide = values.astype(F32)
    mean = jnp.sum(wide, axis=0) / rows
    square = jnp.sum((wide - mean) ** 2, axis=0)
    parts = small_gather_zl(jnp.stack([mean, square]))
    return combine([p[0] for p in parts], [p[1] for p in parts], rows)


def split(vector, pieces):
    out = []
    for _ in range(pieces):
        high = lax.reduce_precision(vector, 8, 7)
        out.append(high.astype(BF16))
        vector = vector - high
    return out


def extra_rows(vectors):
    rows = [piece for vector, pieces in vectors for piece in split(vector, pieces)]
    stacked = jnp.stack(rows)
    return jnp.pad(stacked, ((0, EXTRA - len(rows)),) + ((0, 0),) * (stacked.ndim - 1))


def read_rows(rows, pieces):
    out, at = [], 0
    for count in pieces:
        out.append(sum(rows[at + k] for k in range(count)))
        at += count
    return out


def local(view_one, view_two, proj_weight):
    rows, width = view_one.shape
    n_zl, n_y, n_x = lax.axis_size("zl"), lax.axis_size("y"), lax.axis_size("x")
    n_plane = n_y * n_x
    total_rows = rows * n_zl * n_plane
    blk_i, blk_j = width // n_x, width // n_y
    core = lax.axis_index("c")
    zh = lax.axis_index("zh")

    at_x, at_y = lax.axis_index("x"), lax.axis_index("y")
    rotated_two = rotate(view_two, at_y * blk_j)
    crossed = swap(rotated_two, "zh")
    rotated_one = rotate(view_one, at_x * blk_i)
    plane_rows = n_plane * rows

    def plane_of_two(rotated):
        parts = spread(scatter_columns(rotated, "y"), "x")
        parts = [part.reshape(n_y, 1, rows, blk_j) for part in parts]
        return jnp.concatenate(parts, axis=1).reshape(plane_rows, blk_j)

    own_one = jnp.concatenate(spread(scatter_columns(rotated_one, "x"), "y"), axis=0)
    own = jnp.concatenate([own_one, plane_of_two(rotated_two)], axis=1)
    far_two = plane_of_two(crossed)

    def normalize(values, mean, rstd):
        return ((values.astype(F32) - mean) * rstd).astype(BF16)

    mean, square = moments(own)
    rstd = lax.rsqrt(square / total_rows + EPSILON)
    norm_own = normalize(own, mean, rstd)
    sums_own = jnp.sum(norm_own.astype(F32), axis=0)
    far_stats = swap(jnp.stack([mean[blk_i:], rstd[blk_i:], sums_own[blk_i:]]), "zh")
    sums_one = jnp.concatenate([sums_own[:blk_i], swap(sums_own[:blk_i], "c")])
    sums_two = jnp.concatenate([sums_own[blk_i:], far_stats[2]])
    norm_one = jnp.concatenate([norm_own[:, :blk_i], swap(norm_own[:, :blk_i], "c")], axis=1)
    norm_two = jnp.concatenate([norm_own[:, blk_i:], normalize(far_two, far_stats[0], far_stats[1])], axis=1)
    rstd_one, rstd_two = rstd[:blk_i], rstd[blk_i:]

    tile_i, tile_j = norm_one.shape[1], norm_two.shape[1]
    part = dot(norm_one, norm_two, 0, 0).astype(BF16).reshape(n_zl, tile_i // n_zl, tile_j)
    sums = extra_rows([(sums_one, 2), (sums_two, 2)])
    part = jnp.concatenate([part, jnp.broadcast_to(sums[None], (n_zl,) + sums.shape)], axis=1)
    part = jnp.sum(lax.all_to_all(part, "zl", 0, 0, tiled=True).astype(F32), axis=0)
    slice_i = tile_i // n_zl
    mu_one, mu_two = (v / total_rows for v in read_rows(part[slice_i:], (2, 2)))
    corr = part[:slice_i] / total_rows
    on_diag = lax.axis_index("x") == lax.axis_index("y")

    def diagonal(height, first):
        row_ids = first + lax.broadcasted_iota(jnp.int32, (height, tile_j), 0)
        col_ids = lax.broadcasted_iota(jnp.int32, (height, tile_j), 1)
        return (row_ids == col_ids) & (row_ids < blk_i) & on_diag

    grad = jnp.where(
        diagonal(slice_i, lax.axis_index("zl") * slice_i),
        -2.0 * (1.0 - corr),
        2.0 * OFF_WEIGHT * corr,
    ).astype(BF16)
    grad = gather_zl(grad).reshape(tile_i, tile_j)

    def products(grad):
        wide = grad.astype(F32)
        return wide, wide * jnp.where(diagonal(tile_i, 0), 1.0 + 0.5 * wide, wide / (2.0 * OFF_WEIGHT))

    def delta(normal, upstream, cross, mean_up, rstd):
        return (rstd * (upstream - mean_up - normal.astype(F32) * cross)).astype(BF16)

    def with_extra(piece, extra):
        return jnp.concatenate([piece.reshape(-1, piece.shape[-1]), extra], axis=0)

    wide, product = products(grad)
    cross_one, mean_up_one = jnp.sum(product, axis=1), jnp.sum(wide * mu_two[None, :], axis=1)
    up_one = dot(norm_two, grad, 1, 1)
    other = with_extra(
        up_one[:, blk_i:].astype(BF16), extra_rows([(cross_one[blk_i:], 2), (mean_up_one[blk_i:], 2)])
    )
    other, grad = lax.optimization_barrier((other, grad))
    other = swap(other, "c")

    wide, product = products(grad)
    cross_two, mean_up_two = jnp.sum(product, axis=0), jnp.sum(wide * mu_one[:, None], axis=0)
    up_two = dot(norm_one, grad, 1, 0).astype(BF16).reshape(n_y, n_x, rows, tile_j)

    def for_x(columns):
        extra = extra_rows([(cross_two[columns], 2), (mean_up_two[columns], 2)])
        return [with_extra(up_two[:, k, :, columns], extra) for k in range(n_x)]

    pieces_far, pieces_near = for_x(slice(blk_j, None)), for_x(slice(0, blk_j))
    other, pieces_far, pieces_near = lax.optimization_barrier((other, pieces_far, pieces_near))

    other = other.astype(F32)
    up_one = (up_one[:, :blk_i] + other[:plane_rows]).astype(BF16).reshape(n_y, n_x * rows, blk_i)
    tail = read_rows(other[plane_rows:], (2, 2))
    extra = extra_rows([(cross_one[:blk_i] + tail[0], 2), (mean_up_one[:blk_i] + tail[1], 2)])
    pieces_one = [with_extra(up_one[k], extra) for k in range(n_y)]
    pieces_one, pieces_far = lax.optimization_barrier((pieces_one, pieces_far))

    part_rows = n_y * rows
    far = collect(pieces_far, "x")
    far = with_extra(
        far[:part_rows].astype(BF16), extra_rows([(v, 2) for v in read_rows(far[part_rows:], (2, 2))])
    )
    far, pieces_near = lax.optimization_barrier((far, pieces_near))
    far = swap(far, "zh").astype(F32)

    up_one = collect(pieces_one, "y")
    cross_one, mean_up_one = read_rows(up_one[n_x * rows :], (2, 2))
    delta_one = delta(
        norm_one[: n_x * rows, :blk_i], up_one[: n_x * rows], cross_one, mean_up_one, rstd_one
    )
    delta_one = rotate(gather_columns(delta_one, "x"), ((n_x - at_x) % n_x) * blk_i)

    near = collect(pieces_near, "x")
    up_two = near[:part_rows] + far[:part_rows]
    cross_two, mean_up_two = (
        a + b for a, b in zip(read_rows(near[part_rows:], (2, 2)), read_rows(far[part_rows:], (2, 2)))
    )
    normal = norm_two.reshape(n_y, n_x, rows, tile_j)[:, 0, :, :blk_j].reshape(part_rows, blk_j)
    delta_two = delta(normal, up_two, cross_two, mean_up_two, rstd_two)
    delta_two = rotate(gather_columns(delta_two, "y"), ((n_y - at_y) % n_y) * blk_j)

    weight = proj_weight.reshape(2, 2, width, width)

    def block(half, member):
        return lax.dynamic_slice(weight, (half, member, 0, 0), (1, 1, width, width)).reshape(width, width)

    far_give, far_keep = block(1 - zh, 1 - core), block(1 - zh, core)
    near_give, near_keep = block(zh, 1 - core), block(zh, core)

    def sum_cores(value, keep, give):
        return dot(value, keep, 1, 1) + swap(dot(value, give, 1, 1).astype(BF16), "c").astype(F32)

    far_two = sum_cores(delta_two, far_keep, far_give).astype(BF16)
    far_one = sum_cores(delta_one, far_keep, far_give).astype(BF16)
    far_two, far_one, delta_two, delta_one = lax.optimization_barrier(
        (far_two, far_one, delta_two, delta_one)
    )
    far_two, far_one = swap(far_two, "zh"), swap(far_one, "zh")
    near_two = sum_cores(delta_two, near_keep, near_give)
    near_one = sum_cores(delta_one, near_keep, near_give)
    near_two, near_one = lax.optimization_barrier((near_two, near_one))
    return (
        (near_one + far_one.astype(F32)).astype(BF16),
        (near_two + far_two.astype(F32)).astype(BF16),
    )


def solution(mesh):
    fine = Mesh(mesh.devices.reshape(4, 4, 4, 2, 2), ("zl", "y", "x", "zh", "c"))
    spec = P(("zl", "y", "x"), ("zh", "c"))
    return jax.shard_map(
        local,
        mesh=fine,
        in_specs=(spec, spec, P(None, ("zh", "c"))),
        out_specs=(spec, spec),
        check_vma=False,
    )
```

```python
import jax
import jax.numpy as jnp
from jax import lax
from jax.sharding import Mesh, PartitionSpec as P

OFF_WEIGHT = 0.0125
EPSILON = 1e-05
F32 = jnp.float32
BF16 = jnp.bfloat16
SWAP = [(0, 1), (1, 0)]
EXTRA = 16


def dot(left, right, left_dim, right_dim):
    return lax.dot_general(
        left, right, (((left_dim,), (right_dim,)), ((), ())), preferred_element_type=F32
    )


def swap(value, axis):
    return lax.ppermute(value, axis, SWAP)


def gather_zl(value):
    count = lax.axis_size("zl")
    return lax.all_to_all(
        jnp.broadcast_to(value[None], (count,) + value.shape), "zl", 0, 0, tiled=True
    )


def shift(value, axis, step):
    count = lax.axis_size(axis)
    return lax.ppermute(value, axis, [(i, (i + step) % count) for i in range(count)])


def small_gather_zl(value):
    return [value] + [shift(value, "zl", step) for step in range(1, lax.axis_size("zl"))]


def rotate(value, start):
    return lax.dynamic_slice_in_dim(jnp.concatenate([value, value], axis=1), start, value.shape[1], 1)


def scatter_columns(rotated, axis):
    count = lax.axis_size(axis)
    blocks = jnp.split(rotated, count, axis=1)
    return jnp.concatenate([blocks[0]] + [shift(blocks[k], axis, k) for k in range(1, count)], axis=0)


def gather_columns(stacked, axis):
    count = lax.axis_size(axis)
    blocks = jnp.split(stacked, count, axis=0)
    return jnp.concatenate([blocks[0]] + [shift(blocks[k], axis, -k) for k in range(1, count)], axis=1)


def spread(value, axis):
    return [value] + [shift(value, axis, k) for k in range(1, lax.axis_size(axis))]


def collect(pieces, axis):
    return sum(
        (piece if k == 0 else shift(piece, axis, -k)).astype(F32) for k, piece in enumerate(pieces)
    )


def combine(means, squares, rows):
    mean = sum(means) / len(means)
    return mean, sum(squares) + rows * sum((m - mean) ** 2 for m in means)


def moments(values):
    rows = values.shape[0]
    wide = values.astype(F32)
    mean = jnp.sum(wide, axis=0) / rows
    square = jnp.sum((wide - mean) ** 2, axis=0)
    parts = small_gather_zl(jnp.stack([mean, square]))
    return combine([p[0] for p in parts], [p[1] for p in parts], rows)


def split(vector, pieces):
    out = []
    for _ in range(pieces):
        high = lax.reduce_precision(vector, 8, 7)
        out.append(high.astype(BF16))
        vector = vector - high
    return out


def extra_rows(vectors):
    rows = [piece for vector, pieces in vectors for piece in split(vector, pieces)]
    stacked = jnp.stack(rows)
    return jnp.pad(stacked, ((0, EXTRA - len(rows)),) + ((0, 0),) * (stacked.ndim - 1))


def read_rows(rows, pieces):
    out, at = [], 0
    for count in pieces:
        out.append(sum(rows[at + k] for k in range(count)))
        at += count
    return out


def local(view_one, view_two, proj_weight):
    rows, width = view_one.shape
    n_zl, n_y, n_x = lax.axis_size("zl"), lax.axis_size("y"), lax.axis_size("x")
    n_plane = n_y * n_x
    total_rows = rows * n_zl * n_plane
    blk_i, blk_j = width // n_x, width // n_y
    core = lax.axis_index("c")
    zh = lax.axis_index("zh")

    at_x, at_y = lax.axis_index("x"), lax.axis_index("y")
    rotated_two = rotate(view_two, at_y * blk_j)
    crossed = swap(rotated_two, "zh")
    rotated_one = rotate(view_one, at_x * blk_i)
    plane_rows = n_plane * rows

    def plane_of_two(rotated):
        parts = spread(scatter_columns(rotated, "y"), "x")
        parts = [part.reshape(n_y, 1, rows, blk_j) for part in parts]
        return jnp.concatenate(parts, axis=1).reshape(plane_rows, blk_j)

    own_one = jnp.concatenate(spread(scatter_columns(rotated_one, "x"), "y"), axis=0)
    own = jnp.concatenate([own_one, plane_of_two(rotated_two)], axis=1)
    far_two = plane_of_two(crossed)

    def normalize(values, mean, rstd):
        return ((values.astype(F32) - mean) * rstd).astype(BF16)

    mean, square = moments(own)
    rstd = lax.rsqrt(square / total_rows + EPSILON)
    norm_own = normalize(own, mean, rstd)
    sums_own = jnp.sum(norm_own.astype(F32), axis=0)
    far_stats = swap(jnp.stack([mean[blk_i:], rstd[blk_i:], sums_own[blk_i:]]), "zh")
    sums_one = jnp.concatenate([sums_own[:blk_i], swap(sums_own[:blk_i], "c")])
    sums_two = jnp.concatenate([sums_own[blk_i:], far_stats[2]])
    norm_one = jnp.concatenate([norm_own[:, :blk_i], swap(norm_own[:, :blk_i], "c")], axis=1)
    norm_two = jnp.concatenate([norm_own[:, blk_i:], normalize(far_two, far_stats[0], far_stats[1])], axis=1)
    rstd_one, rstd_two = rstd[:blk_i], rstd[blk_i:]

    tile_i, tile_j = norm_one.shape[1], norm_two.shape[1]
    part = dot(norm_one, norm_two, 0, 0).astype(BF16).reshape(n_zl, tile_i // n_zl, tile_j)
    sums = extra_rows([(sums_one, 2), (sums_two, 2)])
    part = jnp.concatenate([part, jnp.broadcast_to(sums[None], (n_zl,) + sums.shape)], axis=1)
    part = jnp.sum(lax.all_to_all(part, "zl", 0, 0, tiled=True).astype(F32), axis=0)
    slice_i = tile_i // n_zl
    mu_one, mu_two = (v / total_rows for v in read_rows(part[slice_i:], (2, 2)))
    corr = part[:slice_i] / total_rows
    on_diag = lax.axis_index("x") == lax.axis_index("y")

    def diagonal(height, first):
        row_ids = first + lax.broadcasted_iota(jnp.int32, (height, tile_j), 0)
        col_ids = lax.broadcasted_iota(jnp.int32, (height, tile_j), 1)
        return (row_ids == col_ids) & (row_ids < blk_i) & on_diag

    grad = jnp.where(
        diagonal(slice_i, lax.axis_index("zl") * slice_i),
        -2.0 * (1.0 - corr),
        2.0 * OFF_WEIGHT * corr,
    ).astype(BF16)
    grad = gather_zl(grad).reshape(tile_i, tile_j)

    weight = proj_weight.reshape(2, 2, width, width)

    def block(half, member):
        return lax.dynamic_slice(weight, (half, member, 0, 0), (1, 1, width, width)).reshape(width, width)

    far_give, far_keep = block(1 - zh, 1 - core), block(1 - zh, core)
    near_give, near_keep = block(zh, 1 - core), block(zh, core)
    blocks = (far_give, far_keep, near_give, near_keep)
    (far_give, far_keep, near_give, near_keep), grad = lax.optimization_barrier((blocks, grad))

    def products(grad):
        wide = grad.astype(F32)
        return wide, wide * jnp.where(diagonal(tile_i, 0), 1.0 + 0.5 * wide, wide / (2.0 * OFF_WEIGHT))

    def delta(normal, upstream, cross, mean_up, rstd):
        return (rstd * (upstream - mean_up - normal.astype(F32) * cross)).astype(BF16)

    def with_extra(piece, extra):
        return jnp.concatenate([piece.reshape(-1, piece.shape[-1]), extra], axis=0)

    part_rows = n_y * rows

    def for_x(grad, columns):
        wide, product = products(grad)
        cross, mean_up = jnp.sum(product, axis=0), jnp.sum(wide * mu_one[:, None], axis=0)
        extra = extra_rows([(cross[columns], 2), (mean_up[columns], 2)])
        upstream = dot(norm_one, grad[:, columns], 1, 0).astype(BF16).reshape(n_y, n_x, rows, -1)
        return [with_extra(upstream[:, k], extra) for k in range(n_x)]

    pieces_far, grad = lax.optimization_barrier((for_x(grad, slice(blk_j, None)), grad))
    parts_far = [piece if k == 0 else shift(piece, "x", -k) for k, piece in enumerate(pieces_far)]

    wide, product = products(grad)
    cross_one, mean_up_one = jnp.sum(product, axis=1), jnp.sum(wide * mu_two[None, :], axis=1)
    other = with_extra(
        dot(norm_two, grad[blk_i:], 1, 1).astype(BF16),
        extra_rows([(cross_one[blk_i:], 2), (mean_up_one[blk_i:], 2)]),
    )
    other, grad = lax.optimization_barrier((other, grad))
    other = swap(other, "c").astype(F32)
    up_one = (dot(norm_two, grad[:blk_i], 1, 1) + other[:plane_rows]).astype(BF16)
    up_one = up_one.reshape(n_y, n_x * rows, blk_i)
    tail = read_rows(other[plane_rows:], (2, 2))
    extra = extra_rows([(cross_one[:blk_i] + tail[0], 2), (mean_up_one[:blk_i] + tail[1], 2)])
    pieces_one = [with_extra(up_one[k], extra) for k in range(n_y)]
    pieces_near = for_x(grad, slice(0, blk_j))
    parts_far, pieces_near, pieces_one[0] = lax.optimization_barrier((parts_far, pieces_near, pieces_one[0]))
    far = sum(part.astype(F32) for part in parts_far)
    far = with_extra(
        far[:part_rows].astype(BF16), extra_rows([(v, 2) for v in read_rows(far[part_rows:], (2, 2))])
    )
    far = swap(far, "zh").astype(F32)
    near = collect(pieces_near, "x")

    up_one = collect(pieces_one, "y")
    cross_one, mean_up_one = read_rows(up_one[n_x * rows :], (2, 2))
    delta_one = delta(
        norm_one[: n_x * rows, :blk_i], up_one[: n_x * rows], cross_one, mean_up_one, rstd_one
    )
    delta_one = rotate(gather_columns(delta_one, "x"), ((n_x - at_x) % n_x) * blk_i)

    up_two = near[:part_rows] + far[:part_rows]
    cross_two, mean_up_two = (
        a + b for a, b in zip(read_rows(near[part_rows:], (2, 2)), read_rows(far[part_rows:], (2, 2)))
    )
    normal = norm_two.reshape(n_y, n_x, rows, tile_j)[:, 0, :, :blk_j].reshape(part_rows, blk_j)
    delta_two = delta(normal, up_two, cross_two, mean_up_two, rstd_two)
    delta_two = rotate(gather_columns(delta_two, "y"), ((n_y - at_y) % n_y) * blk_j)

    def input_grad(value):
        far = dot(value, far_keep, 1, 1) + swap(dot(value, far_give, 1, 1).astype(BF16), "c").astype(F32)
        far = swap(far.astype(BF16), "zh").astype(F32)
        near = dot(value, near_keep, 1, 1) + swap(dot(value, near_give, 1, 1).astype(BF16), "c").astype(F32)
        return (near + far).astype(BF16)

    grad_two = input_grad(delta_two)
    return input_grad(delta_one), grad_two


def solution(mesh):
    fine = Mesh(mesh.devices.reshape(4, 4, 4, 2, 2), ("zl", "y", "x", "zh", "c"))
    spec = P(("zl", "y", "x"), ("zh", "c"))
    return jax.shard_map(
        local,
        mesh=fine,
        in_specs=(spec, spec, P(None, ("zh", "c"))),
        out_specs=(spec, spec),
        check_vma=False,
    )
```

```python
import jax
import jax.numpy as jnp
from jax import lax
from jax.sharding import Mesh, PartitionSpec as P

OFF_WEIGHT = 0.0125
EPSILON = 1e-05
F32 = jnp.float32
BF16 = jnp.bfloat16
SWAP = [(0, 1), (1, 0)]
EXTRA = 16


def dot(left, right, left_dim, right_dim):
    return lax.dot_general(
        left, right, (((left_dim,), (right_dim,)), ((), ())), preferred_element_type=F32
    )


def swap(value, axis):
    return lax.ppermute(value, axis, SWAP)


def gather_zl(value):
    count = lax.axis_size("zl")
    return lax.all_to_all(
        jnp.broadcast_to(value[None], (count,) + value.shape), "zl", 0, 0, tiled=True
    )


def shift(value, axis, step):
    count = lax.axis_size(axis)
    return lax.ppermute(value, axis, [(i, (i + step) % count) for i in range(count)])


def small_gather_zl(value):
    return [value] + [shift(value, "zl", step) for step in range(1, lax.axis_size("zl"))]


def rotate(value, start):
    return lax.dynamic_slice_in_dim(jnp.concatenate([value, value], axis=1), start, value.shape[1], 1)


def scatter_columns(rotated, axis):
    count = lax.axis_size(axis)
    blocks = jnp.split(rotated, count, axis=1)
    return jnp.concatenate([blocks[0]] + [shift(blocks[k], axis, k) for k in range(1, count)], axis=0)


def gather_columns(stacked, axis):
    count = lax.axis_size(axis)
    blocks = jnp.split(stacked, count, axis=0)
    return jnp.concatenate([blocks[0]] + [shift(blocks[k], axis, -k) for k in range(1, count)], axis=1)


def spread(value, axis):
    return [value] + [shift(value, axis, k) for k in range(1, lax.axis_size(axis))]


def collect(pieces, axis):
    return sum(
        (piece if k == 0 else shift(piece, axis, -k)).astype(F32) for k, piece in enumerate(pieces)
    )


def combine(means, squares, rows):
    mean = sum(means) / len(means)
    return mean, sum(squares) + rows * sum((m - mean) ** 2 for m in means)


def moments(values):
    rows = values.shape[0]
    wide = values.astype(F32)
    mean = jnp.sum(wide, axis=0) / rows
    square = jnp.sum((wide - mean) ** 2, axis=0)
    parts = small_gather_zl(jnp.stack([mean, square]))
    return combine([p[0] for p in parts], [p[1] for p in parts], rows)


def split(vector, pieces):
    out = []
    for _ in range(pieces):
        high = lax.reduce_precision(vector, 8, 7)
        out.append(high.astype(BF16))
        vector = vector - high
    return out


def extra_rows(vectors):
    rows = [piece for vector, pieces in vectors for piece in split(vector, pieces)]
    stacked = jnp.stack(rows)
    return jnp.pad(stacked, ((0, EXTRA - len(rows)),) + ((0, 0),) * (stacked.ndim - 1))


def read_rows(rows, pieces):
    out, at = [], 0
    for count in pieces:
        out.append(sum(rows[at + k] for k in range(count)))
        at += count
    return out


def local(view_one, view_two, proj_weight):
    rows, width = view_one.shape
    n_zl, n_y, n_x = lax.axis_size("zl"), lax.axis_size("y"), lax.axis_size("x")
    n_plane = n_y * n_x
    total_rows = rows * n_zl * n_plane
    blk_i, blk_j = width // n_x, width // n_y
    core = lax.axis_index("c")
    zh = lax.axis_index("zh")

    at_x, at_y = lax.axis_index("x"), lax.axis_index("y")
    rotated_two = rotate(view_two, at_y * blk_j)
    crossed = rotate(swap(view_two, "zh"), at_y * blk_j)
    rotated_one = rotate(view_one, at_x * blk_i)
    plane_rows = n_plane * rows

    def plane_of_two(rotated):
        parts = spread(scatter_columns(rotated, "y"), "x")
        parts = [part.reshape(n_y, 1, rows, blk_j) for part in parts]
        return jnp.concatenate(parts, axis=1).reshape(plane_rows, blk_j)

    own_one = jnp.concatenate(spread(scatter_columns(rotated_one, "x"), "y"), axis=0)
    own = jnp.concatenate([own_one, plane_of_two(rotated_two)], axis=1)
    far_two = plane_of_two(crossed)

    def normalize(values, mean, rstd):
        return ((values.astype(F32) - mean) * rstd).astype(BF16)

    mean, square = moments(own)
    rstd = lax.rsqrt(square / total_rows + EPSILON)
    norm_own = normalize(own, mean, rstd)
    sums_own = jnp.sum(norm_own.astype(F32), axis=0)
    far_stats = swap(jnp.stack([mean[blk_i:], rstd[blk_i:], sums_own[blk_i:]]), "zh")
    sums_one = jnp.concatenate([sums_own[:blk_i], swap(sums_own[:blk_i], "c")])
    sums_two = jnp.concatenate([sums_own[blk_i:], far_stats[2]])
    norm_one = jnp.concatenate([norm_own[:, :blk_i], swap(norm_own[:, :blk_i], "c")], axis=1)
    norm_two = jnp.concatenate([norm_own[:, blk_i:], normalize(far_two, far_stats[0], far_stats[1])], axis=1)
    rstd_one, rstd_two = rstd[:blk_i], rstd[blk_i:]

    tile_i, tile_j = norm_one.shape[1], norm_two.shape[1]
    part = dot(norm_one, norm_two, 0, 0).astype(BF16).reshape(n_zl, tile_i // n_zl, tile_j)
    sums = extra_rows([(sums_one, 2), (sums_two, 2)])
    part = jnp.concatenate([part, jnp.broadcast_to(sums[None], (n_zl,) + sums.shape)], axis=1)
    part = jnp.sum(lax.all_to_all(part, "zl", 0, 0, tiled=True).astype(F32), axis=0)
    slice_i = tile_i // n_zl
    mu_one, mu_two = (v / total_rows for v in read_rows(part[slice_i:], (2, 2)))
    corr = part[:slice_i] / total_rows
    on_diag = lax.axis_index("x") == lax.axis_index("y")

    def diagonal(height, first):
        row_ids = first + lax.broadcasted_iota(jnp.int32, (height, tile_j), 0)
        col_ids = lax.broadcasted_iota(jnp.int32, (height, tile_j), 1)
        return (row_ids == col_ids) & (row_ids < blk_i) & on_diag

    grad = jnp.where(
        diagonal(slice_i, lax.axis_index("zl") * slice_i),
        -2.0 * (1.0 - corr),
        2.0 * OFF_WEIGHT * corr,
    ).astype(BF16)
    grad = gather_zl(grad).reshape(tile_i, tile_j)

    def products(grad):
        wide = grad.astype(F32)
        return wide, wide * jnp.where(diagonal(tile_i, 0), 1.0 + 0.5 * wide, wide / (2.0 * OFF_WEIGHT))

    def delta(normal, upstream, cross, mean_up, rstd):
        return (rstd * (upstream - mean_up - normal.astype(F32) * cross)).astype(BF16)

    def with_extra(piece, extra):
        return jnp.concatenate([piece.reshape(-1, piece.shape[-1]), extra], axis=0)

    wide, product = products(grad)
    cross_one, mean_up_one = jnp.sum(product, axis=1), jnp.sum(wide * mu_two[None, :], axis=1)
    up_one = dot(norm_two, grad, 1, 1)
    other = with_extra(
        up_one[:, blk_i:].astype(BF16), extra_rows([(cross_one[blk_i:], 2), (mean_up_one[blk_i:], 2)])
    )
    other, grad = lax.optimization_barrier((other, grad))
    other = swap(other, "c")

    wide, product = products(grad)
    cross_two, mean_up_two = jnp.sum(product, axis=0), jnp.sum(wide * mu_one[:, None], axis=0)
    up_two = dot(norm_one, grad, 1, 0).astype(BF16).reshape(n_y, n_x, rows, tile_j)

    def for_x(columns):
        extra = extra_rows([(cross_two[columns], 2), (mean_up_two[columns], 2)])
        return [with_extra(up_two[:, k, :, columns], extra) for k in range(n_x)]

    pieces_far, pieces_near = for_x(slice(blk_j, None)), for_x(slice(0, blk_j))
    other, pieces_far, pieces_near = lax.optimization_barrier((other, pieces_far, pieces_near))

    other = other.astype(F32)
    up_one = (up_one[:, :blk_i] + other[:plane_rows]).astype(BF16).reshape(n_y, n_x * rows, blk_i)
    tail = read_rows(other[plane_rows:], (2, 2))
    extra = extra_rows([(cross_one[:blk_i] + tail[0], 2), (mean_up_one[:blk_i] + tail[1], 2)])
    pieces_one = [with_extra(up_one[k], extra) for k in range(n_y)]
    pieces_one, pieces_far = lax.optimization_barrier((pieces_one, pieces_far))

    part_rows = n_y * rows
    far = collect(pieces_far, "x")
    far = with_extra(
        far[:part_rows].astype(BF16), extra_rows([(v, 2) for v in read_rows(far[part_rows:], (2, 2))])
    )
    far, pieces_near = lax.optimization_barrier((far, pieces_near))
    far = swap(far, "zh").astype(F32)

    up_one = collect(pieces_one, "y")
    cross_one, mean_up_one = read_rows(up_one[n_x * rows :], (2, 2))
    delta_one = delta(
        norm_one[: n_x * rows, :blk_i], up_one[: n_x * rows], cross_one, mean_up_one, rstd_one
    )
    delta_one = rotate(gather_columns(delta_one, "x"), ((n_x - at_x) % n_x) * blk_i)

    near = collect(pieces_near, "x")
    up_two = near[:part_rows] + far[:part_rows]
    cross_two, mean_up_two = (
        a + b for a, b in zip(read_rows(near[part_rows:], (2, 2)), read_rows(far[part_rows:], (2, 2)))
    )
    normal = norm_two.reshape(n_y, n_x, rows, tile_j)[:, 0, :, :blk_j].reshape(part_rows, blk_j)
    delta_two = delta(normal, up_two, cross_two, mean_up_two, rstd_two)
    delta_two = rotate(gather_columns(delta_two, "y"), ((n_y - at_y) % n_y) * blk_j)

    weight = proj_weight.reshape(2, 2, width, width)

    def block(half, member):
        return lax.dynamic_slice(weight, (half, member, 0, 0), (1, 1, width, width)).reshape(width, width)

    far_give, far_keep = block(1 - zh, 1 - core), block(1 - zh, core)
    near_give, near_keep = block(zh, 1 - core), block(zh, core)

    def input_grad(value):
        far = dot(value, far_keep, 1, 1) + swap(dot(value, far_give, 1, 1).astype(BF16), "c").astype(F32)
        far = swap(far.astype(BF16), "zh").astype(F32)
        near = dot(value, near_keep, 1, 1) + swap(dot(value, near_give, 1, 1).astype(BF16), "c").astype(F32)
        return (near + far).astype(BF16)

    grad_two = input_grad(delta_two)
    return input_grad(delta_one), grad_two


def solution(mesh):
    fine = Mesh(mesh.devices.reshape(4, 4, 4, 2, 2), ("zl", "y", "x", "zh", "c"))
    spec = P(("zl", "y", "x"), ("zh", "c"))
    return jax.shard_map(
        local,
        mesh=fine,
        in_specs=(spec, spec, P(None, ("zh", "c"))),
        out_specs=(spec, spec),
        check_vma=False,
    )
```
